32 devices in a mesh: pair: 8 (over z, y), rep: 4 (over x, core).
Axes of the slice: x: 2, y: 2, z: 4, core: 2. Of those that a mesh axis runs over, the one named last changes fastest.
Arguments:
- tau_ao: bfloat16 [512, 8192], P('pair'), may hold values from -6 to 6
- slab_sizes: int32 [32], replicated, may hold values from 1 to 512, 8192 in all
- integrals: bfloat16 [32, 512, 1024], P('pair', 'rep'), may hold values from -0.0625 to 0.0625
- transform: float32 [1024, 512], replicated, may hold values from -0.1875 to 0.1875
Outputs:
- ladder_mo: float32 [512, 512], P('pair', 'rep')
The draws below stay inside these ranges and needn't reach their ends.
Inputs may be any that keep to these rules, and one draw needn't show every extreme that they name: `slab_sizes`: the sizes sum to 8192 and the largest equals 512.
All inputs are finite; a program needn't handle non-finite values.
Results may differ from the reference program's by a relative error of at most 0.0003.
Values may be sent and summed in bfloat16 or wider, within the bound.
A program may use at most 128 MiB of HBM per device.

```python
import math
import jax
import jax.numpy as jnp
import numpy as np
from jax import lax

SLAB_CAP = 512
NK = 1024
NV = 512
NPAIRS = 512
NSLAB = 32
NQ = 8192


def block_levels(rng, extent, pieces, least, largest):
    factor_of = 1.0
    for axis_at, parts in pieces:
        steps = jax.random.uniform(jax.random.fold_in(jax.random.fold_in(rng, 6), axis_at), (parts,), jnp.float32, least / len(pieces), largest / len(pieces))
        factor_of = factor_of * jnp.repeat(jnp.exp(steps), extent[axis_at] // parts).reshape((-1,) + (1,) * (len(extent) - 1 - axis_at))
    return factor_of


def profile(amount, total, limit, lean):
    portions = [(1 << 20) // math.isqrt(grade ** lean) + 1 for grade in range(2, amount + 1)]
    rest, given = total - limit - (amount - 1), [1] * (amount - 1)
    while rest > 0:
        candidates = [i for i in range(amount - 1) if given[i] < limit]
        whole, left = sum([portions[i] for i in candidates]), rest
        for i in candidates:
            addition = min(limit - given[i], max(1, left * portions[i] // whole), rest)
            given[i] = given[i] + addition
            rest = rest - addition
    return np.array([limit] + given)


def ragged(rng, amount, total, reach, slope):
    if amount == 2:
        one = jax.random.randint(rng, (), max(1, total - reach), min(reach, total - 1) + 1)
        return jnp.stack([one, total - one])
    tallies = jnp.asarray(profile(amount, total, reach, slope), jnp.int32)
    twos = (amount - 1) // 2
    source_of, sink = tallies[1:1 + 2 * twos:2], tallies[2:2 + 2 * twos:2]
    slack = jnp.minimum(source_of - 1, reach - sink)
    shifted = jax.random.randint(jax.random.fold_in(rng, 1), (twos,), 0, 1 << 20) % (slack + 1)
    tallies = tallies.at[1:1 + 2 * twos:2].set(source_of - shifted).at[2:2 + 2 * twos:2].set(sink + shifted)
    return tallies[jax.random.permutation(jax.random.fold_in(rng, 2), amount)]


def normal_values(key, shape, scale, reach, split=(), kind=jnp.bfloat16):
    result = scale * jax.random.normal(key, shape, jnp.float32)
    if split:
        result = result * block_levels(key, shape, split, -0.22, 0.18)
    return jnp.clip(result, -reach, reach).astype(kind)


def setup_inputs(seed: int = 0) -> dict:
    splits = jax.random.split(jax.random.key(seed), 5)
    return {
        "tau_ao": normal_values(splits[0], (NPAIRS, NQ), 1.0, 6.0, ((0, 8),)),
        "slab_sizes": ragged(splits[1], NSLAB, NQ, SLAB_CAP, 2).astype(jnp.int32),
        "integrals": normal_values(splits[2], (NSLAB, SLAB_CAP, NK), NQ ** -0.5, 0.0625, ((0, 8), (1, 4))),
        "transform": normal_values(splits[3], (NK, NV), NK ** -0.5, 0.1875, (), jnp.float32),
    }


def reference(tau_ao, slab_sizes, integrals, transform):
    sizes_int = slab_sizes.astype(jnp.int32)
    offsets = (jnp.cumsum(sizes_int) - sizes_int).astype(jnp.int32)
    slot_index = jnp.arange(SLAB_CAP, dtype=jnp.int32)

    def add_slab(ladder, entry):
        first_col, col_count, slab_block = entry
        columns = jnp.clip(first_col + slot_index, 0, NQ - 1).astype(jnp.int32)
        picked = jnp.take(tau_ao, columns, axis=1)
        picked = jnp.where(slot_index[None, :] < col_count, picked, jnp.zeros_like(picked))
        product = jnp.dot(picked.astype(jnp.float32), slab_block.astype(jnp.float32), precision=lax.Precision.HIGHEST)
        return ladder + product, None

    ladder, unused = lax.scan(add_slab, jnp.zeros((NPAIRS, NK), jnp.float32), (offsets, sizes_int, integrals))
    return jnp.dot(ladder, transform, precision=lax.Precision.HIGHEST)
```

```python
import functools

import jax
import jax.numpy as jnp
from jax import lax
from jax.experimental import pallas as pl
from jax.experimental.pallas import tpu as pltpu
from jax.sharding import PartitionSpec as P

MESH = pl.DeviceIdType.MESH
LANES = 128


def hop(slot, n):
    u = slot - 1
    h, odd = lax.div(u + 1, 2), lax.rem(u, 2)
    return n // 2 + h * (2 * odd - 1)


def pick_kernel(n, slabs, sizes, tau, target, offsets):
    me, rep = lax.axis_index("pair"), lax.axis_index("rep")
    pairs, packed = tau.shape
    rows = target.shape[2] // slabs

    def add_up(s, total):
        offsets[s] = total
        return total + sizes[s]

    lax.fori_loop(0, sizes.shape[0], add_up, jnp.int32(0))
    places = lax.broadcasted_iota(jnp.int32, (pairs, rows), 1) + rep * rows

    @pl.loop(0, n)
    def _(slot):
        dest = jnp.where(slot == 0, me, lax.rem(me + hop(slot, n), n))
        for q in range(slabs):
            slab = dest * slabs + q
            start = jnp.minimum(offsets[slab] + rep * rows, packed - 1)
            base = jnp.minimum(lax.div(start, LANES) * LANES, packed - 2 * LANES)
            window = tau[:, pl.ds(pl.multiple_of(base, LANES), 2 * LANES)].astype(jnp.float32)
            turned = pltpu.roll(window, 2 * LANES - (start - base), 1)[:, :rows]
            kept = jnp.where(places < sizes[slab], turned, 0.0)
            target[slot, :, q * rows : (q + 1) * rows] = kept.astype(jnp.bfloat16)


def kernel(
    n, amps_out, integrals_in, transform_in, out,
    integrals, transform, t_hi, t_lo, w_hi, w_lo, amps, part, core_in, x_in, done, back,
    load_sem, amps_send, amps_recv, core_send, core_recv, x_send, x_recv, back_send, back_recv,
):
    me, rep = lax.axis_index("pair"), lax.axis_index("rep")
    hi, lo = lax.div(rep, 2), lax.rem(rep, 2)
    near, far = hi * 2 + (1 - lo), (1 - hi) * 2 + lo
    slabs, rows, width = integrals.shape

    load_own = pltpu.make_async_copy(amps_out.at[0], amps.at[0], load_sem.at[0])
    load_integrals = pltpu.make_async_copy(integrals_in, integrals, load_sem.at[1])
    load_transform = pltpu.make_async_copy(transform_in, transform, load_sem.at[2])
    load_own.start()
    load_transform.start()
    load_integrals.start()

    barrier = pltpu.get_barrier_semaphore()

    @pl.loop(1, n)
    def _(slot):
        other = lax.rem(me + hop(slot, n), n)
        pl.semaphore_signal(barrier, inc=1, device_id=(other, rep), device_id_type=MESH)

    pl.semaphore_signal(barrier, inc=1, device_id=(me, near), device_id_type=MESH)
    pl.semaphore_signal(barrier, inc=1, device_id=(me, far), device_id_type=MESH)

    def send_amps(slot):
        other = lax.rem(me + hop(slot, n), n)
        return pltpu.make_async_remote_copy(
            src_ref=amps_out.at[slot], dst_ref=amps.at[slot],
            send_sem=amps_send.at[slot], recv_sem=amps_recv.at[slot],
            device_id=(other, rep), device_id_type=MESH,
        )

    def send_core(slot):
        return pltpu.make_async_remote_copy(
            src_ref=part.at[slot, 1 - lo], dst_ref=core_in.at[slot],
            send_sem=core_send.at[slot], recv_sem=core_recv.at[slot],
            device_id=(me, near), device_id_type=MESH,
        )

    def send_x(slot):
        return pltpu.make_async_remote_copy(
            src_ref=part.at[slot, lo, 1 - hi], dst_ref=x_in.at[slot],
            send_sem=x_send.at[slot], recv_sem=x_recv.at[slot],
            device_id=(me, far), device_id_type=MESH,
        )

    def send_back(slot):
        owner = lax.rem(me + n - hop(slot, n), n)
        return pltpu.make_async_remote_copy(
            src_ref=done.at[slot], dst_ref=back.at[slot],
            send_sem=back_send.at[slot], recv_sem=back_recv.at[slot],
            device_id=(owner, rep), device_id_type=MESH,
        )

    pl.semaphore_wait(barrier, n + 1)

    @pl.loop(1, n)
    def _(slot):
        send_amps(slot).start()

    load_transform.wait()

    @pl.loop(0, width, step=256)
    def _(k):
        block = transform[pl.ds(k, 256), :]
        high = block.astype(jnp.bfloat16)
        t_hi[pl.ds(k, 256), :] = high
        t_lo[pl.ds(k, 256), :] = (block - high.astype(jnp.float32)).astype(jnp.bfloat16)

    load_integrals.wait()
    for at in range(0, t_hi.shape[1], 2 * LANES):
        flat = integrals[...].reshape(slabs * rows, width)
        columns = slice(at, at + 2 * LANES)
        w = jnp.dot(flat, t_lo[:, columns], preferred_element_type=jnp.float32)
        w += jnp.dot(flat, t_hi[:, columns], preferred_element_type=jnp.float32)
        high = w.astype(jnp.bfloat16)
        w_hi[:, columns] = high
        w_lo[:, columns] = (w - high.astype(jnp.float32)).astype(jnp.bfloat16)

    load_own.wait()

    @pl.loop(0, n + 2)
    def _(step):
        @pl.when(jnp.logical_and(step >= 1, step < n))
        def _():
            send_amps(step).wait_recv()

        @pl.when(step < n)
        def _():
            block = amps[step]
            for h in range(2):
                columns = slice(h * 2 * LANES, (h + 1) * 2 * LANES)
                p = jnp.dot(block, w_lo[:, columns], preferred_element_type=jnp.float32)
                p += jnp.dot(block, w_hi[:, columns], preferred_element_type=jnp.float32)
                part[step, 0, h] = p[:, :LANES]
                part[step, 1, h] = p[:, LANES:]
            send_core(step).start()

        @pl.when(jnp.logical_and(step >= 1, step <= n))
        def _():
            slot = step - 1
            send_core(slot).wait_recv()
            part[slot, lo, 1 - hi] = part[slot, lo, 1 - hi] + core_in[slot, 1 - hi]
            send_x(slot).start()

        @pl.when(step >= 2)
        def _():
            slot = step - 2
            send_x(slot).wait_recv()
            done[slot] = part[slot, lo, hi] + core_in[slot, hi] + x_in[slot]

            @pl.when(slot >= 1)
            def _():
                send_back(slot).start()

    out[...] = done[0]

    @pl.loop(1, n)
    def _(slot):
        send_back(slot).wait_recv()
        out[...] = out[...] + back[slot]

    @pl.loop(0, n)
    def _(slot):
        @pl.when(slot >= 1)
        def _():
            send_amps(slot).wait_send()
            send_back(slot).wait_send()

        send_core(slot).wait_send()
        send_x(slot).wait_send()


def solution(mesh):
    n, reps = mesh.shape["pair"], mesh.shape["rep"]

    def body(tau_ao, slab_sizes, integrals, transform):
        pairs, packed = tau_ao.shape
        slabs, rows, width = integrals.shape
        virtuals = transform.shape[1]
        assert reps == 4 and rows == LANES and virtuals == reps * LANES
        slots = slabs * rows
        bf, f32, dma = jnp.bfloat16, jnp.float32, pltpu.SemaphoreType.DMA
        flops = 4 * slots * width * virtuals + 4 * n * pairs * slots * virtuals
        amps = pl.pallas_call(
            functools.partial(pick_kernel, n, slabs),
            out_shape=jax.ShapeDtypeStruct((n, pairs, slots), bf),
            in_specs=[
                pl.BlockSpec(memory_space=pltpu.SMEM),
                pl.BlockSpec(memory_space=pltpu.VMEM),
            ],
            out_specs=pl.BlockSpec(memory_space=pltpu.VMEM),
            scratch_shapes=[pltpu.SMEM((slab_sizes.shape[0],), jnp.int32)],
            compiler_params=pltpu.CompilerParams(vmem_limit_bytes=48 * 1024 * 1024),
            cost_estimate=pl.CostEstimate(flops=0, bytes_accessed=2 << 20, transcendentals=0),
        )(slab_sizes, tau_ao)
        return pl.pallas_call(
            functools.partial(kernel, n),
            out_shape=jax.ShapeDtypeStruct((pairs, LANES), f32),
            in_specs=[pl.BlockSpec(memory_space=pl.ANY)] * 3,
            out_specs=pl.BlockSpec(memory_space=pltpu.VMEM),
            scratch_shapes=[
                pltpu.VMEM((slabs, rows, width), bf),
                pltpu.VMEM((width, virtuals), f32),
                pltpu.VMEM((width, virtuals), bf),
                pltpu.VMEM((width, virtuals), bf),
                pltpu.VMEM((slots, virtuals), bf),
                pltpu.VMEM((slots, virtuals), bf),
                pltpu.VMEM((n, pairs, slots), bf),
                pltpu.VMEM((n, 2, 2, pairs, LANES), f32),
                pltpu.VMEM((n, 2, pairs, LANES), f32),
                pltpu.VMEM((n, pairs, LANES), f32),
                pltpu.VMEM((n, pairs, LANES), f32),
                pltpu.VMEM((n, pairs, LANES), f32),
                dma((3,)),
            ] + [dma((n,))] * 8,
            compiler_params=pltpu.CompilerParams(
                collective_id=0, has_side_effects=True, vmem_limit_bytes=56 * 1024 * 1024
            ),
            cost_estimate=pl.CostEstimate(flops=flops, bytes_accessed=4 << 20, transcendentals=0),
        )(amps, integrals, transform)

    return jax.shard_map(
        body,
        mesh=mesh,
        in_specs=(P("pair", None), P(), P("pair", "rep", None), P()),
        out_specs=P("pair", "rep"),
        check_vma=False,
    )
```

```python
import functools

import jax
import jax.numpy as jnp
from jax import lax
from jax.experimental import pallas as pl
from jax.experimental.pallas import tpu as pltpu
from jax.sharding import PartitionSpec as P

MESH = pl.DeviceIdType.MESH
LANES = 128


def partner(me, slot, n):
    other, bit = 0, 1
    while bit < n:
        other += lax.rem(lax.div(me, bit) + lax.div(slot, bit), 2) * bit
        bit *= 2
    return other


def pick_kernel(n, slabs, sizes, tau, target, offsets):
    me, rep = lax.axis_index("pair"), lax.axis_index("rep")
    pairs, packed = tau.shape
    rows = target.shape[2] // slabs

    def add_up(s, total):
        offsets[s] = total
        return total + sizes[s]

    lax.fori_loop(0, sizes.shape[0], add_up, jnp.int32(0))
    places = lax.broadcasted_iota(jnp.int32, (pairs, rows), 1) + rep * rows

    @pl.loop(0, n)
    def _(slot):
        dest = partner(me, slot, n)
        for q in range(slabs):
            slab = dest * slabs + q
            start = jnp.minimum(offsets[slab] + rep * rows, packed - 1)
            base = jnp.minimum(lax.div(start, LANES) * LANES, packed - 2 * LANES)
            window = tau[:, pl.ds(pl.multiple_of(base, LANES), 2 * LANES)].astype(jnp.float32)
            turned = pltpu.roll(window, lax.rem(2 * LANES - (start - base), 2 * LANES), 1)[:, :rows]
            kept = jnp.where(places < sizes[slab], turned, 0.0)
            target[slot, :, q * rows : (q + 1) * rows] = kept.astype(jnp.bfloat16)


def kernel(
    n, amps_out, integrals_in, transform_in, out,
    integrals, transform, t_hi, t_lo, w_hi, w_lo, amps, part, core_in, x_in, done, back,
    load_sem, amps_send, amps_recv, core_send, core_recv, x_send, x_recv, back_send, back_recv,
):
    me, rep = lax.axis_index("pair"), lax.axis_index("rep")
    hi, lo = lax.div(rep, 2), lax.rem(rep, 2)
    near, far = hi * 2 + (1 - lo), (1 - hi) * 2 + lo
    slabs, rows, width = integrals.shape

    load_own = pltpu.make_async_copy(amps_out.at[0], amps.at[0], load_sem.at[0])
    load_integrals = pltpu.make_async_copy(integrals_in, integrals, load_sem.at[1])
    load_transform = pltpu.make_async_copy(transform_in, transform, load_sem.at[2])
    load_own.start()
    load_transform.start()
    load_integrals.start()

    barrier = pltpu.get_barrier_semaphore()

    @pl.loop(1, n)
    def _(slot):
        other = partner(me, slot, n)
        pl.semaphore_signal(barrier, inc=1, device_id=(other, rep), device_id_type=MESH)

    pl.semaphore_signal(barrier, inc=1, device_id=(me, near), device_id_type=MESH)
    pl.semaphore_signal(barrier, inc=1, device_id=(me, far), device_id_type=MESH)

    def send_amps(slot):
        other = partner(me, slot, n)
        return pltpu.make_async_remote_copy(
            src_ref=amps_out.at[slot], dst_ref=amps.at[slot],
            send_sem=amps_send.at[slot], recv_sem=amps_recv.at[slot],
            device_id=(other, rep), device_id_type=MESH,
        )

    def send_core(slot):
        return pltpu.make_async_remote_copy(
            src_ref=part.at[slot, 1 - lo], dst_ref=core_in.at[slot],
            send_sem=core_send.at[slot], recv_sem=core_recv.at[slot],
            device_id=(me, near), device_id_type=MESH,
        )

    def send_x(slot):
        return pltpu.make_async_remote_copy(
            src_ref=part.at[slot, lo, 1 - hi], dst_ref=x_in.at[slot],
            send_sem=x_send.at[slot], recv_sem=x_recv.at[slot],
            device_id=(me, far), device_id_type=MESH,
        )

    def send_back(slot):
        owner = partner(me, slot, n)
        return pltpu.make_async_remote_copy(
            src_ref=done.at[slot], dst_ref=back.at[slot],
            send_sem=back_send.at[slot], recv_sem=back_recv.at[slot],
            device_id=(owner, rep), device_id_type=MESH,
        )

    pl.semaphore_wait(barrier, n + 1)

    half = n // 2
    for slot in (half, half + 1):
        send_amps(jnp.int32(slot)).start()

    @pl.loop(1, half)
    def _(slot):
        send_amps(slot).start()

    load_transform.wait()

    @pl.loop(0, width, step=256)
    def _(k):
        block = transform[pl.ds(k, 256), :]
        high = block.astype(jnp.bfloat16)
        t_hi[pl.ds(k, 256), :] = high
        t_lo[pl.ds(k, 256), :] = (block - high.astype(jnp.float32)).astype(jnp.bfloat16)

    load_integrals.wait()
    for at in range(0, t_hi.shape[1], 2 * LANES):
        flat = integrals[...].reshape(slabs * rows, width)
        columns = slice(at, at + 2 * LANES)
        w = jnp.dot(flat, t_lo[:, columns], preferred_element_type=jnp.float32)
        w += jnp.dot(flat, t_hi[:, columns], preferred_element_type=jnp.float32)
        high = w.astype(jnp.bfloat16)
        w_hi[:, columns] = high
        w_lo[:, columns] = (w - high.astype(jnp.float32)).astype(jnp.bfloat16)

    load_own.wait()

    @pl.loop(0, n + 2)
    def _(step):
        @pl.when(jnp.logical_and(step >= 1, step < n))
        def _():
            send_amps(step).wait_recv()

        @pl.when(jnp.logical_and(step >= half, step < n - 2))
        def _():
            send_amps(step).wait_send()
            send_amps(step + 2).start()

        @pl.when(step < n)
        def _():
            block = amps[step]
            for h in range(2):
                columns = slice(h * 2 * LANES, (h + 1) * 2 * LANES)
                p = jnp.dot(block, w_lo[:, columns], preferred_element_type=jnp.float32)
                p += jnp.dot(block, w_hi[:, columns], preferred_element_type=jnp.float32)
                part[step, 0, h] = p[:, :LANES]
                part[step, 1, h] = p[:, LANES:]
            send_core(step).start()

        @pl.when(jnp.logical_and(step >= 1, step <= n))
        def _():
            slot = step - 1
            send_core(slot).wait_recv()
            part[slot, lo, 1 - hi] = part[slot, lo, 1 - hi] + core_in[slot, 1 - hi]
            send_x(slot).start()

        @pl.when(step >= 2)
        def _():
            slot = step - 2
            send_x(slot).wait_recv()
            done[slot] = part[slot, lo, hi] + core_in[slot, hi] + x_in[slot]

            @pl.when(slot >= 1)
            def _():
                send_back(slot).start()

    out[...] = done[0]

    @pl.loop(1, n)
    def _(slot):
        send_back(slot).wait_recv()
        out[...] = out[...] + back[slot]

    @pl.loop(0, n)
    def _(slot):
        @pl.when(slot >= 1)
        def _():
            send_back(slot).wait_send()

        @pl.when(jnp.logical_or(jnp.logical_and(slot >= 1, slot < half), slot >= n - 2))
        def _():
            send_amps(slot).wait_send()

        send_core(slot).wait_send()
        send_x(slot).wait_send()


def solution(mesh):
    n, reps = mesh.shape["pair"], mesh.shape["rep"]

    def body(tau_ao, slab_sizes, integrals, transform):
        pairs, packed = tau_ao.shape
        slabs, rows, width = integrals.shape
        virtuals = transform.shape[1]
        assert reps == 4 and rows == LANES and virtuals == reps * LANES
        slots = slabs * rows
        bf, f32, dma = jnp.bfloat16, jnp.float32, pltpu.SemaphoreType.DMA
        flops = 4 * slots * width * virtuals + 4 * n * pairs * slots * virtuals
        amps = pl.pallas_call(
            functools.partial(pick_kernel, n, slabs),
            out_shape=jax.ShapeDtypeStruct((n, pairs, slots), bf),
            in_specs=[
                pl.BlockSpec(memory_space=pltpu.SMEM),
                pl.BlockSpec(memory_space=pltpu.VMEM),
            ],
            out_specs=pl.BlockSpec(memory_space=pltpu.VMEM),
            scratch_shapes=[pltpu.SMEM((slab_sizes.shape[0],), jnp.int32)],
            compiler_params=pltpu.CompilerParams(vmem_limit_bytes=48 * 1024 * 1024),
            cost_estimate=pl.CostEstimate(flops=0, bytes_accessed=2 << 20, transcendentals=0),
        )(slab_sizes, tau_ao)
        return pl.pallas_call(
            functools.partial(kernel, n),
            out_shape=jax.ShapeDtypeStruct((pairs, LANES), f32),
            in_specs=[pl.BlockSpec(memory_space=pl.ANY)] + [pl.BlockSpec(memory_space=pltpu.HBM)] * 2,
            out_specs=pl.BlockSpec(memory_space=pltpu.VMEM),
            scratch_shapes=[
                pltpu.VMEM((slabs, rows, width), bf),
                pltpu.VMEM((width, virtuals), f32),
                pltpu.VMEM((width, virtuals), bf),
                pltpu.VMEM((width, virtuals), bf),
                pltpu.VMEM((slots, virtuals), bf),
                pltpu.VMEM((slots, virtuals), bf),
                pltpu.VMEM((n, pairs, slots), bf),
                pltpu.VMEM((n, 2, 2, pairs, LANES), f32),
                pltpu.VMEM((n, 2, pairs, LANES), f32),
                pltpu.VMEM((n, pairs, LANES), f32),
                pltpu.VMEM((n, pairs, LANES), f32),
                pltpu.VMEM((n, pairs, LANES), f32),
                dma((3,)),
            ] + [dma((n,))] * 8,
            compiler_params=pltpu.CompilerParams(
                collective_id=0, has_side_effects=True, vmem_limit_bytes=56 * 1024 * 1024
            ),
            cost_estimate=pl.CostEstimate(flops=flops, bytes_accessed=4 << 20, transcendentals=0),
        )(amps, integrals, transform)

    return jax.shard_map(
        body,
        mesh=mesh,
        in_specs=(P("pair", None), P(), P("pair", "rep", None), P()),
        out_specs=P("pair", "rep"),
        check_vma=False,
    )
```

```python
import functools

import jax
import jax.numpy as jnp
from jax import lax
from jax.experimental import pallas as pl
from jax.experimental.pallas import tpu as pltpu
from jax.sharding import PartitionSpec as P

MESH = pl.DeviceIdType.MESH
LANES = 128


def partner(me, slot, n):
    other, bit = 0, 1
    while bit < n:
        other += lax.rem(lax.div(me, bit) + lax.div(slot, bit), 2) * bit
        bit *= 2
    return other


def pick_kernel(n, slabs, sizes, tau, target, offsets):
    me, rep = lax.axis_index("pair"), lax.axis_index("rep")
    pairs, packed = tau.shape
    rows = target.shape[2] // slabs

    def add_up(s, total):
        offsets[s] = total
        return total + sizes[s]

    lax.fori_loop(0, sizes.shape[0], add_up, jnp.int32(0))
    places = lax.broadcasted_iota(jnp.int32, (pairs, rows), 1) + rep * rows

    @pl.loop(0, n)
    def _(slot):
        dest = partner(me, slot, n)
        for q in range(slabs):
            slab = dest * slabs + q
            start = jnp.minimum(offsets[slab] + rep * rows, packed - 1)
            base = jnp.minimum(lax.div(start, LANES) * LANES, packed - 2 * LANES)
            window = tau[:, pl.ds(pl.multiple_of(base, LANES), 2 * LANES)].astype(jnp.float32)
            turned = pltpu.roll(window, lax.rem(2 * LANES - (start - base), 2 * LANES), 1)[:, :rows]
            kept = jnp.where(places < sizes[slab], turned, 0.0)
            target[slot, :, q * rows : (q + 1) * rows] = kept.astype(jnp.bfloat16)


def kernel(
    n, amps_out, integrals_in, transform_in, out,
    integrals, transform, t_hi, t_lo, w_hi, w_lo, amps, part, core_in, x_in, done, y_in, back,
    load_sem, amps_send, amps_recv, core_send, core_recv, x_send, x_recv, y_send, y_recv, back_send, back_recv,
):
    me, rep = lax.axis_index("pair"), lax.axis_index("rep")
    hi, lo = lax.div(rep, 2), lax.rem(rep, 2)
    near, far = hi * 2 + (1 - lo), (1 - hi) * 2 + lo
    slabs, rows, width = integrals.shape

    load_own = pltpu.make_async_copy(amps_out.at[0], amps.at[0], load_sem.at[0])
    load_integrals = pltpu.make_async_copy(integrals_in, integrals, load_sem.at[1])
    load_transform = pltpu.make_async_copy(transform_in, transform, load_sem.at[2])
    load_own.start()
    load_transform.start()
    load_integrals.start()

    barrier = pltpu.get_barrier_semaphore()

    @pl.loop(1, n)
    def _(slot):
        other = partner(me, slot, n)
        pl.semaphore_signal(barrier, inc=1, device_id=(other, rep), device_id_type=MESH)

    pl.semaphore_signal(barrier, inc=1, device_id=(me, near), device_id_type=MESH)
    pl.semaphore_signal(barrier, inc=1, device_id=(me, far), device_id_type=MESH)

    def send_amps(slot):
        other = partner(me, slot, n)
        return pltpu.make_async_remote_copy(
            src_ref=amps_out.at[slot], dst_ref=amps.at[slot],
            send_sem=amps_send.at[slot], recv_sem=amps_recv.at[slot],
            device_id=(other, rep), device_id_type=MESH,
        )

    def send_core(slot):
        return pltpu.make_async_remote_copy(
            src_ref=part.at[slot, 1 - lo], dst_ref=core_in.at[slot],
            send_sem=core_send.at[slot], recv_sem=core_recv.at[slot],
            device_id=(me, near), device_id_type=MESH,
        )

    def send_x(slot):
        return pltpu.make_async_remote_copy(
            src_ref=part.at[slot, lo, 1 - hi], dst_ref=x_in.at[slot],
            send_sem=x_send.at[slot], recv_sem=x_recv.at[slot],
            device_id=(me, far), device_id_type=MESH,
        )

    def send_y(slot):
        return pltpu.make_async_remote_copy(
            src_ref=done.at[slot], dst_ref=y_in.at[slot],
            send_sem=y_send.at[slot], recv_sem=y_recv.at[slot],
            device_id=(partner(me, 1, n), rep), device_id_type=MESH,
        )

    def send_back(duo):
        return pltpu.make_async_remote_copy(
            src_ref=done.at[2 * duo], dst_ref=back.at[duo],
            send_sem=back_send.at[duo], recv_sem=back_recv.at[duo],
            device_id=(partner(me, 2 * duo, n), rep), device_id_type=MESH,
        )

    pl.semaphore_wait(barrier, n + 1)

    half = n // 2
    for slot in (half, half + 1):
        send_amps(jnp.int32(slot)).start()

    @pl.loop(1, half)
    def _(slot):
        send_amps(slot).start()

    load_transform.wait()

    @pl.loop(0, width, step=256)
    def _(k):
        block = transform[pl.ds(k, 256), :]
        high = block.astype(jnp.bfloat16)
        t_hi[pl.ds(k, 256), :] = high
        t_lo[pl.ds(k, 256), :] = (block - high.astype(jnp.float32)).astype(jnp.bfloat16)

    load_integrals.wait()
    for at in range(0, t_hi.shape[1], 2 * LANES):
        flat = integrals[...].reshape(slabs * rows, width)
        columns = slice(at, at + 2 * LANES)
        w = jnp.dot(flat, t_lo[:, columns], preferred_element_type=jnp.float32)
        w += jnp.dot(flat, t_hi[:, columns], preferred_element_type=jnp.float32)
        high = w.astype(jnp.bfloat16)
        w_hi[:, columns] = high
        w_lo[:, columns] = (w - high.astype(jnp.float32)).astype(jnp.bfloat16)

    load_own.wait()

    @pl.loop(0, n + 3)
    def _(step):
        @pl.when(jnp.logical_and(step >= 1, step < n))
        def _():
            send_amps(step).wait_recv()

        @pl.when(jnp.logical_and(step >= half, step < n - 2))
        def _():
            send_amps(step).wait_send()
            send_amps(step + 2).start()

        @pl.when(step < n)
        def _():
            block = amps[step]
            for h in range(2):
                columns = slice(h * 2 * LANES, (h + 1) * 2 * LANES)
                p = jnp.dot(block, w_lo[:, columns], preferred_element_type=jnp.float32)
                p += jnp.dot(block, w_hi[:, columns], preferred_element_type=jnp.float32)
                part[step, 0, h] = p[:, :LANES]
                part[step, 1, h] = p[:, LANES:]
            send_core(step).start()

        @pl.when(jnp.logical_and(step >= 1, step <= n))
        def _():
            slot = step - 1
            send_core(slot).wait_recv()
            part[slot, lo, 1 - hi] = part[slot, lo, 1 - hi] + core_in[slot, 1 - hi]
            send_x(slot).start()

        @pl.when(jnp.logical_and(step >= 2, step <= n + 1))
        def _():
            slot = step - 2
            send_x(slot).wait_recv()
            done[slot] = part[slot, lo, hi] + core_in[slot, hi] + x_in[slot]

            @pl.when(lax.rem(slot, 2) == 1)
            def _():
                send_y(slot).start()

        @pl.when(jnp.logical_and(step >= 4, lax.rem(step, 2) == 0))
        def _():
            slot = step - 3
            send_y(slot).wait_recv()
            done[slot - 1] = done[slot - 1] + y_in[slot]

            @pl.when(slot >= 3)
            def _():
                send_back(lax.div(slot, 2)).start()

    out[...] = done[0]

    @pl.loop(1, half)
    def _(duo):
        send_back(duo).wait_recv()
        out[...] = out[...] + back[duo]

    @pl.loop(0, n)
    def _(slot):
        @pl.when(jnp.logical_or(jnp.logical_and(slot >= 1, slot < half), slot >= n - 2))
        def _():
            send_amps(slot).wait_send()

        @pl.when(lax.rem(slot, 2) == 1)
        def _():
            send_y(slot).wait_send()

        send_core(slot).wait_send()
        send_x(slot).wait_send()

    @pl.loop(1, half)
    def _(duo):
        send_back(duo).wait_send()


def solution(mesh):
    n, reps = mesh.shape["pair"], mesh.shape["rep"]

    def body(tau_ao, slab_sizes, integrals, transform):
        pairs, packed = tau_ao.shape
        slabs, rows, width = integrals.shape
        virtuals = transform.shape[1]
        assert reps == 4 and rows == LANES and virtuals == reps * LANES
        slots = slabs * rows
        bf, f32, dma = jnp.bfloat16, jnp.float32, pltpu.SemaphoreType.DMA
        flops = 4 * slots * width * virtuals + 4 * n * pairs * slots * virtuals
        amps = pl.pallas_call(
            functools.partial(pick_kernel, n, slabs),
            out_shape=jax.ShapeDtypeStruct((n, pairs, slots), bf),
            in_specs=[
                pl.BlockSpec(memory_space=pltpu.SMEM),
                pl.BlockSpec(memory_space=pltpu.VMEM),
            ],
            out_specs=pl.BlockSpec(memory_space=pltpu.VMEM),
            scratch_shapes=[pltpu.SMEM((slab_sizes.shape[0],), jnp.int32)],
            compiler_params=pltpu.CompilerParams(vmem_limit_bytes=16 << 20),
            cost_estimate=pl.CostEstimate(flops=0, bytes_accessed=2 << 20, transcendentals=0),
        )(slab_sizes, tau_ao)
        return pl.pallas_call(
            functools.partial(kernel, n),
            out_shape=jax.ShapeDtypeStruct((pairs, LANES), f32),
            in_specs=[pl.BlockSpec(memory_space=pltpu.VMEM)] + [pl.BlockSpec(memory_space=pltpu.HBM)] * 2,
            out_specs=pl.BlockSpec(memory_space=pltpu.VMEM),
            scratch_shapes=[
                pltpu.VMEM((slabs, rows, width), bf),
                pltpu.VMEM((width, virtuals), f32),
                pltpu.VMEM((width, virtuals), bf),
                pltpu.VMEM((width, virtuals), bf),
                pltpu.VMEM((slots, virtuals), bf),
                pltpu.VMEM((slots, virtuals), bf),
                pltpu.VMEM((n, pairs, slots), bf),
                pltpu.VMEM((n, 2, 2, pairs, LANES), f32),
                pltpu.VMEM((n, 2, pairs, LANES), f32),
                pltpu.VMEM((n, pairs, LANES), f32),
                pltpu.VMEM((n, pairs, LANES), f32),
                pltpu.VMEM((n, pairs, LANES), f32),
                pltpu.VMEM((n // 2, pairs, LANES), f32),
                dma((3,)),
            ] + [dma((n,))] * 8 + [dma((n // 2,))] * 2,
            compiler_params=pltpu.CompilerParams(
                collective_id=0, has_side_effects=True, vmem_limit_bytes=(14 << 20) + n * (9 << 16)
            ),
            cost_estimate=pl.CostEstimate(flops=flops, bytes_accessed=4 << 20, transcendentals=0),
        )(amps, integrals, transform)

    return jax.shard_map(
        body,
        mesh=mesh,
        in_specs=(P("pair", None), P(), P("pair", "rep", None), P()),
        out_specs=P("pair", "rep"),
        check_vma=False,
    )
```

```python
import functools

import jax
import jax.numpy as jnp
from jax import lax
from jax.experimental import pallas as pl
from jax.experimental.pallas import tpu as pltpu
from jax.sharding import PartitionSpec as P

MESH = pl.DeviceIdType.MESH
LANES = 128


def partner(me, slot, n):
    other, bit = 0, 1
    while bit < n:
        other += lax.rem(lax.div(me, bit) + lax.div(slot, bit), 2) * bit
        bit *= 2
    return other


def pick_kernel(n, slabs, sizes, tau, target, offsets):
    me, rep = lax.axis_index("pair"), lax.axis_index("rep")
    pairs, packed = tau.shape
    rows = target.shape[2] // slabs

    def add_up(s, total):
        offsets[s] = total
        return total + sizes[s]

    lax.fori_loop(0, sizes.shape[0], add_up, jnp.int32(0))
    places = lax.broadcasted_iota(jnp.int32, (pairs, rows), 1) + rep * rows

    @pl.loop(0, n)
    def _(slot):
        dest = partner(me, slot, n)
        for q in range(slabs):
            slab = dest * slabs + q
            start = jnp.minimum(offsets[slab] + rep * rows, packed - 1)
            base = jnp.minimum(lax.div(start, LANES) * LANES, packed - 2 * LANES)
            window = tau[:, pl.ds(pl.multiple_of(base, LANES), 2 * LANES)].astype(jnp.float32)
            turned = pltpu.roll(window, lax.rem(2 * LANES - (start - base), 2 * LANES), 1)[:, :rows]
            kept = jnp.where(places < sizes[slab], turned, 0.0)
            target[slot, :, q * rows : (q + 1) * rows] = kept.astype(jnp.bfloat16)


def kernel(
    n, amps_out, integrals_in, transform_in, out,
    integrals, transform, t_hi, t_lo, w_hi, w_lo, amps, part, core_in, x_in, done, back,
    load_sem, amps_send, amps_recv, core_send, core_recv, x_send, x_recv, back_send, back_recv,
):
    me, rep = lax.axis_index("pair"), lax.axis_index("rep")
    hi, lo = lax.div(rep, 2), lax.rem(rep, 2)
    near, far = hi * 2 + (1 - lo), (1 - hi) * 2 + lo
    slabs, rows, width = integrals.shape

    load_own = pltpu.make_async_copy(amps_out.at[0], amps.at[0], load_sem.at[0])
    load_integrals = pltpu.make_async_copy(integrals_in, integrals, load_sem.at[1])
    load_transform = pltpu.make_async_copy(transform_in, transform, load_sem.at[2])
    load_own.start()
    load_transform.start()
    load_integrals.start()

    barrier = pltpu.get_barrier_semaphore()

    @pl.loop(1, n)
    def _(slot):
        other = partner(me, slot, n)
        pl.semaphore_signal(barrier, inc=1, device_id=(other, rep), device_id_type=MESH)

    pl.semaphore_signal(barrier, inc=1, device_id=(me, near), device_id_type=MESH)
    pl.semaphore_signal(barrier, inc=1, device_id=(me, far), device_id_type=MESH)

    def send_amps(slot):
        other = partner(me, slot, n)
        return pltpu.make_async_remote_copy(
            src_ref=amps_out.at[slot], dst_ref=amps.at[slot],
            send_sem=amps_send.at[slot], recv_sem=amps_recv.at[slot],
            device_id=(other, rep), device_id_type=MESH,
        )

    def send_core(slot):
        return pltpu.make_async_remote_copy(
            src_ref=part.at[slot, 1 - lo], dst_ref=core_in.at[slot],
            send_sem=core_send.at[slot], recv_sem=core_recv.at[slot],
            device_id=(me, near), device_id_type=MESH,
        )

    def send_x(slot):
        return pltpu.make_async_remote_copy(
            src_ref=part.at[slot, lo, 1 - hi], dst_ref=x_in.at[slot],
            send_sem=x_send.at[slot], recv_sem=x_recv.at[slot],
            device_id=(me, far), device_id_type=MESH,
        )

    def send_back(slot):
        owner = partner(me, slot, n)
        return pltpu.make_async_remote_copy(
            src_ref=done.at[slot], dst_ref=back.at[slot],
            send_sem=back_send.at[slot], recv_sem=back_recv.at[slot],
            device_id=(owner, rep), device_id_type=MESH,
        )

    pl.semaphore_wait(barrier, n + 1)

    half = n // 2
    for slot in (half, half + 1):
        send_amps(jnp.int32(slot)).start()

    @pl.loop(1, half)
    def _(slot):
        send_amps(slot).start()

    load_transform.wait()

    @pl.loop(0, width, step=256)
    def _(k):
        block = transform[pl.ds(k, 256), :]
        high = block.astype(jnp.bfloat16)
        t_hi[pl.ds(k, 256), :] = high
        t_lo[pl.ds(k, 256), :] = (block - high.astype(jnp.float32)).astype(jnp.bfloat16)

    load_integrals.wait()
    for at in range(0, t_hi.shape[1], 2 * LANES):
        flat = integrals[...].reshape(slabs * rows, width)
        columns = slice(at, at + 2 * LANES)
        w = jnp.dot(flat, t_lo[:, columns], preferred_element_type=jnp.float32)
        w += jnp.dot(flat, t_hi[:, columns], preferred_element_type=jnp.float32)
        high = w.astype(jnp.bfloat16)
        w_hi[:, columns] = high
        w_lo[:, columns] = (w - high.astype(jnp.float32)).astype(jnp.bfloat16)

    load_own.wait()

    def multiply(first, last):
        @pl.loop(first, last)
        def _(slot):
            @pl.when(slot >= 1)
            def _():
                send_amps(slot).wait_recv()

            @pl.when(jnp.logical_and(slot >= half, slot < n - 2))
            def _():
                send_amps(slot).wait_send()
                send_amps(slot + 2).start()

            block = amps[slot]
            for h in range(2):
                columns = slice(h * 2 * LANES, (h + 1) * 2 * LANES)
                p = jnp.dot(block, w_lo[:, columns], preferred_element_type=jnp.float32)
                p += jnp.dot(block, w_hi[:, columns], preferred_element_type=jnp.float32)
                part[slot, 0, h] = p[:, :LANES]
                part[slot, 1, h] = p[:, LANES:]
            send_core(slot).start()

    def sum_core(first, last):
        @pl.loop(first, last)
        def _(slot):
            send_core(slot).wait_recv()
            part[slot, lo, 1 - hi] = part[slot, lo, 1 - hi] + core_in[slot, 1 - hi]
            send_x(slot).start()

    def sum_x(first, last):
        @pl.loop(first, last)
        def _(slot):
            send_x(slot).wait_recv()
            done[slot] = part[slot, lo, hi] + core_in[slot, hi] + x_in[slot]

            @pl.when(slot >= 1)
            def _():
                send_back(slot).start()

    groups = [(0, half)] + [(at, at + 2) for at in range(half, n, 2)]
    for at, group in enumerate(groups):
        multiply(*group)
        if at:
            sum_x(*groups[at - 1])
        sum_core(*group)
    sum_x(*groups[-1])

    out[...] = done[0]

    @pl.loop(1, n)
    def _(slot):
        send_back(slot).wait_recv()
        out[...] = out[...] + back[slot]

    @pl.loop(0, n)
    def _(slot):
        @pl.when(slot >= 1)
        def _():
            send_back(slot).wait_send()

        @pl.when(jnp.logical_or(jnp.logical_and(slot >= 1, slot < half), slot >= n - 2))
        def _():
            send_amps(slot).wait_send()

        send_core(slot).wait_send()
        send_x(slot).wait_send()


def solution(mesh):
    n, reps = mesh.shape["pair"], mesh.shape["rep"]

    def body(tau_ao, slab_sizes, integrals, transform):
        pairs, packed = tau_ao.shape
        slabs, rows, width = integrals.shape
        virtuals = transform.shape[1]
        assert reps == 4 and rows == LANES and virtuals == reps * LANES
        slots = slabs * rows
        bf, f32, dma = jnp.bfloat16, jnp.float32, pltpu.SemaphoreType.DMA
        flops = 4 * slots * width * virtuals + 4 * n * pairs * slots * virtuals
        amps = pl.pallas_call(
            functools.partial(pick_kernel, n, slabs),
            out_shape=jax.ShapeDtypeStruct((n, pairs, slots), bf),
            in_specs=[
                pl.BlockSpec(memory_space=pltpu.SMEM),
                pl.BlockSpec(memory_space=pltpu.VMEM),
            ],
            out_specs=pl.BlockSpec(memory_space=pltpu.VMEM),
            scratch_shapes=[pltpu.SMEM((slab_sizes.shape[0],), jnp.int32)],
            compiler_params=pltpu.CompilerParams(vmem_limit_bytes=48 * 1024 * 1024),
            cost_estimate=pl.CostEstimate(flops=0, bytes_accessed=2 << 20, transcendentals=0),
        )(slab_sizes, tau_ao)
        return pl.pallas_call(
            functools.partial(kernel, n),
            out_shape=jax.ShapeDtypeStruct((pairs, LANES), f32),
            in_specs=[pl.BlockSpec(memory_space=pltpu.VMEM)] + [pl.BlockSpec(memory_space=pltpu.HBM)] * 2,
            out_specs=pl.BlockSpec(memory_space=pltpu.VMEM),
            scratch_shapes=[
                pltpu.VMEM((slabs, rows, width), bf),
                pltpu.VMEM((width, virtuals), f32),
                pltpu.VMEM((width, virtuals), bf),
                pltpu.VMEM((width, virtuals), bf),
                pltpu.VMEM((slots, virtuals), bf),
                pltpu.VMEM((slots, virtuals), bf),
                pltpu.VMEM((n, pairs, slots), bf),
                pltpu.VMEM((n, 2, 2, pairs, LANES), f32),
                pltpu.VMEM((n, 2, pairs, LANES), f32),
                pltpu.VMEM((n, pairs, LANES), f32),
                pltpu.VMEM((n, pairs, LANES), f32),
                pltpu.VMEM((n, pairs, LANES), f32),
                dma((3,)),
            ] + [dma((n,))] * 8,
            compiler_params=pltpu.CompilerParams(
                collective_id=0, has_side_effects=True, vmem_limit_bytes=211 << 18
            ),
            cost_estimate=pl.CostEstimate(flops=flops, bytes_accessed=4 << 20, transcendentals=0),
        )(amps, integrals, transform)

    return jax.shard_map(
        body,
        mesh=mesh,
        in_specs=(P("pair", None), P(), P("pair", "rep", None), P()),
        out_specs=P("pair", "rep"),
        check_vma=False,
    )
```

```python
import functools

import jax
import jax.numpy as jnp
from jax import lax
from jax.experimental import pallas as pl
from jax.experimental.pallas import tpu as pltpu
from jax.sharding import PartitionSpec as P

MESH = pl.DeviceIdType.MESH
LANES = 128


def partner(me, slot, n):
    other, bit = 0, 1
    while bit < n:
        other += lax.rem(lax.div(me, bit) + lax.div(slot, bit), 2) * bit
        bit *= 2
    return other


def pick_kernel(n, slabs, sizes_in, tau_in, target, offsets, sizes, tau, load_sem):
    me, rep = lax.axis_index("pair"), lax.axis_index("rep")
    pairs, packed = tau.shape
    rows = target.shape[2] // slabs

    load_sizes = pltpu.make_async_copy(sizes_in, sizes, load_sem.at[0])
    load_tau = pltpu.make_async_copy(tau_in, tau, load_sem.at[1])
    load_sizes.start()
    load_tau.start()
    load_sizes.wait()

    def add_up(s, total):
        offsets[s] = total
        return total + sizes[s]

    lax.fori_loop(0, sizes.shape[0], add_up, jnp.int32(0))
    places = lax.broadcasted_iota(jnp.int32, (pairs, rows), 1) + rep * rows
    load_tau.wait()

    @pl.loop(0, n)
    def _(slot):
        dest = partner(me, slot, n)
        for q in range(slabs):
            slab = dest * slabs + q
            start = jnp.minimum(offsets[slab] + rep * rows, packed - 1)
            base = jnp.minimum(lax.div(start, LANES) * LANES, packed - 2 * LANES)
            window = tau[:, pl.ds(pl.multiple_of(base, LANES), 2 * LANES)].astype(jnp.float32)
            turned = pltpu.roll(window, lax.rem(2 * LANES - (start - base), 2 * LANES), 1)[:, :rows]
            kept = jnp.where(places < sizes[slab], turned, 0.0)
            target[slot, :, q * rows : (q + 1) * rows] = kept.astype(jnp.bfloat16)


def kernel(
    n, amps_out, integrals_in, transform_in, out,
    integrals, transform, t_hi, t_lo, w_hi, w_lo, amps, part, core_in, x_in, done, back,
    load_sem, amps_send, amps_recv, core_send, core_recv, x_send, x_recv, back_send, back_recv,
):
    me, rep = lax.axis_index("pair"), lax.axis_index("rep")
    hi, lo = lax.div(rep, 2), lax.rem(rep, 2)
    near, far = hi * 2 + (1 - lo), (1 - hi) * 2 + lo
    slabs, rows, width = integrals.shape

    load_own = pltpu.make_async_copy(amps_out.at[0], amps.at[0], load_sem.at[0])
    load_integrals = pltpu.make_async_copy(integrals_in, integrals, load_sem.at[1])
    load_transform = pltpu.make_async_copy(transform_in, transform, load_sem.at[2])
    load_own.start()
    load_transform.start()
    load_integrals.start()

    barrier = pltpu.get_barrier_semaphore()

    @pl.loop(1, n)
    def _(slot):
        other = partner(me, slot, n)
        pl.semaphore_signal(barrier, inc=1, device_id=(other, rep), device_id_type=MESH)

    pl.semaphore_signal(barrier, inc=1, device_id=(me, near), device_id_type=MESH)
    pl.semaphore_signal(barrier, inc=1, device_id=(me, far), device_id_type=MESH)

    def send_amps(slot):
        other = partner(me, slot, n)
        return pltpu.make_async_remote_copy(
            src_ref=amps_out.at[slot], dst_ref=amps.at[slot],
            send_sem=amps_send.at[slot], recv_sem=amps_recv.at[slot],
            device_id=(other, rep), device_id_type=MESH,
        )

    def send_core(slot):
        return pltpu.make_async_remote_copy(
            src_ref=part.at[slot, 1 - lo], dst_ref=core_in.at[slot],
            send_sem=core_send.at[slot], recv_sem=core_recv.at[slot],
            device_id=(me, near), device_id_type=MESH,
        )

    def send_x(slot):
        return pltpu.make_async_remote_copy(
            src_ref=part.at[slot, lo, 1 - hi], dst_ref=x_in.at[slot],
            send_sem=x_send.at[slot], recv_sem=x_recv.at[slot],
            device_id=(me, far), device_id_type=MESH,
        )

    def send_back(slot):
        owner = partner(me, slot, n)
        return pltpu.make_async_remote_copy(
            src_ref=done.at[slot], dst_ref=back.at[slot],
            send_sem=back_send.at[slot], recv_sem=back_recv.at[slot],
            device_id=(owner, rep), device_id_type=MESH,
        )

    pl.semaphore_wait(barrier, n + 1)

    half = n // 2

    @pl.loop(half, n)
    def _(slot):
        send_amps(slot).start()

    @pl.loop(1, half)
    def _(slot):
        send_amps(slot).start()

    load_transform.wait()

    @pl.loop(0, width, step=256)
    def _(k):
        block = transform[pl.ds(k, 256), :]
        high = block.astype(jnp.bfloat16)
        t_hi[pl.ds(k, 256), :] = high
        t_lo[pl.ds(k, 256), :] = (block - high.astype(jnp.float32)).astype(jnp.bfloat16)

    load_integrals.wait()
    for at in range(0, t_hi.shape[1], 2 * LANES):
        flat = integrals[...].reshape(slabs * rows, width)
        columns = slice(at, at + 2 * LANES)
        w = jnp.dot(flat, t_lo[:, columns], preferred_element_type=jnp.float32)
        w += jnp.dot(flat, t_hi[:, columns], preferred_element_type=jnp.float32)
        high = w.astype(jnp.bfloat16)
        w_hi[:, columns] = high
        w_lo[:, columns] = (w - high.astype(jnp.float32)).astype(jnp.bfloat16)

    load_own.wait()

    def multiply(first, last):
        @pl.loop(first, last)
        def _(slot):
            @pl.when(slot >= 1)
            def _():
                send_amps(slot).wait_recv()

            block = amps[slot]
            for h in range(2):
                columns = slice(h * 2 * LANES, (h + 1) * 2 * LANES)
                p = jnp.dot(block, w_lo[:, columns], preferred_element_type=jnp.float32)
                p += jnp.dot(block, w_hi[:, columns], preferred_element_type=jnp.float32)
                part[slot, 0, h] = p[:, :LANES]
                part[slot, 1, h] = p[:, LANES:]
            send_core(slot).start()

    def sum_core(first, last):
        @pl.loop(first, last)
        def _(slot):
            send_core(slot).wait_recv()
            part[slot, lo, 1 - hi] = part[slot, lo, 1 - hi] + core_in[slot, 1 - hi]
            send_x(slot).start()

    def sum_x(first, last):
        @pl.loop(first, last)
        def _(slot):
            send_x(slot).wait_recv()
            done[slot] = part[slot, lo, hi] + core_in[slot, hi] + x_in[slot]

            @pl.when(slot >= 1)
            def _():
                send_back(slot).start()

    groups = [(0, half)] + [(at, at + 2) for at in range(half, n, 2)]
    for at, group in enumerate(groups):
        multiply(*group)
        if at:
            sum_x(*groups[at - 1])
        sum_core(*group)
    sum_x(*groups[-1])

    out[...] = done[0]

    @pl.loop(1, n)
    def _(slot):
        send_back(slot).wait_recv()
        out[...] = out[...] + back[slot]

    @pl.loop(0, n)
    def _(slot):
        @pl.when(slot >= 1)
        def _():
            send_amps(slot).wait_send()
            send_back(slot).wait_send()

        send_core(slot).wait_send()
        send_x(slot).wait_send()


def solution(mesh):
    n, reps = mesh.shape["pair"], mesh.shape["rep"]

    def body(tau_ao, slab_sizes, integrals, transform):
        pairs, packed = tau_ao.shape
        slabs, rows, width = integrals.shape
        virtuals = transform.shape[1]
        assert reps == 4 and rows == LANES and virtuals == reps * LANES
        slots = slabs * rows
        bf, f32, dma = jnp.bfloat16, jnp.float32, pltpu.SemaphoreType.DMA
        flops = 4 * slots * width * virtuals + 4 * n * pairs * slots * virtuals
        amps = pl.pallas_call(
            functools.partial(pick_kernel, n, slabs),
            out_shape=jax.ShapeDtypeStruct((n, pairs, slots), bf),
            in_specs=[pl.BlockSpec(memory_space=pltpu.HBM)] * 2,
            out_specs=pl.BlockSpec(memory_space=pltpu.VMEM),
            scratch_shapes=[pltpu.SMEM((slab_sizes.shape[0],), jnp.int32)] * 2 + [
                pltpu.VMEM((pairs, packed), bf),
                dma((2,)),
            ],
            compiler_params=pltpu.CompilerParams(vmem_limit_bytes=211 << 18),
            cost_estimate=pl.CostEstimate(flops=0, bytes_accessed=2 << 20, transcendentals=0),
        )(slab_sizes, tau_ao)
        return pl.pallas_call(
            functools.partial(kernel, n),
            out_shape=jax.ShapeDtypeStruct((pairs, LANES), f32),
            in_specs=[pl.BlockSpec(memory_space=pltpu.VMEM)] + [pl.BlockSpec(memory_space=pltpu.HBM)] * 2,
            out_specs=pl.BlockSpec(memory_space=pltpu.VMEM),
            scratch_shapes=[
                pltpu.VMEM((slabs, rows, width), bf),
                pltpu.VMEM((width, virtuals), f32),
                pltpu.VMEM((width, virtuals), bf),
                pltpu.VMEM((width, virtuals), bf),
                pltpu.VMEM((slots, virtuals), bf),
                pltpu.VMEM((slots, virtuals), bf),
                pltpu.VMEM((n, pairs, slots), bf),
                pltpu.VMEM((n, 2, 2, pairs, LANES), f32),
                pltpu.VMEM((n, 2, pairs, LANES), f32),
                pltpu.VMEM((n, pairs, LANES), f32),
                pltpu.VMEM((n, pairs, LANES), f32),
                pltpu.VMEM((n, pairs, LANES), f32),
                dma((3,)),
            ] + [dma((n,))] * 8,
            compiler_params=pltpu.CompilerParams(
                collective_id=0, has_side_effects=True, vmem_limit_bytes=211 << 18
            ),
            cost_estimate=pl.CostEstimate(flops=flops, bytes_accessed=4 << 20, transcendentals=0),
        )(amps, integrals, transform)

    return jax.shard_map(
        body,
        mesh=mesh,
        in_specs=(P("pair", None), P(), P("pair", "rep", None), P()),
        out_specs=P("pair", "rep"),
        check_vma=False,
    )
```

```python
import functools

import jax
import jax.numpy as jnp
from jax import lax
from jax.experimental import pallas as pl
from jax.experimental.pallas import tpu as pltpu
from jax.sharding import PartitionSpec as P

MESH = pl.DeviceIdType.MESH
LANES = 128
AHEAD = 3


def partner(me, slot, n):
    other, bit = 0, 1
    while bit < n:
        other += lax.rem(lax.div(me, bit) + lax.div(slot, bit), 2) * bit
        bit *= 2
    return other


def pick_kernel(n, slabs, sizes_in, tau_in, target, offsets, sizes, tau, load_sem):
    me, rep = lax.axis_index("pair"), lax.axis_index("rep")
    pairs, packed = tau.shape
    rows = target.shape[2] // slabs

    load_sizes = pltpu.make_async_copy(sizes_in, sizes, load_sem.at[0])
    load_tau = pltpu.make_async_copy(tau_in, tau, load_sem.at[1])
    load_sizes.start()
    load_tau.start()
    load_sizes.wait()

    def add_up(s, total):
        offsets[s] = total
        return total + sizes[s]

    lax.fori_loop(0, sizes.shape[0], add_up, jnp.int32(0))
    places = lax.broadcasted_iota(jnp.int32, (pairs, rows), 1) + rep * rows
    load_tau.wait()

    @pl.loop(0, n)
    def _(slot):
        dest = partner(me, slot, n)
        for q in range(slabs):
            slab = dest * slabs + q
            start = jnp.minimum(offsets[slab] + rep * rows, packed - 1)
            base = jnp.minimum(lax.div(start, LANES) * LANES, packed - 2 * LANES)
            window = tau[:, pl.ds(pl.multiple_of(base, LANES), 2 * LANES)].astype(jnp.float32)
            turned = pltpu.roll(window, lax.rem(2 * LANES - (start - base), 2 * LANES), 1)[:, :rows]
            kept = jnp.where(places < sizes[slab], turned, 0.0)
            target[slot, :, q * rows : (q + 1) * rows] = kept.astype(jnp.bfloat16)


def kernel(
    n, amps_out, integrals_in, transform_in, out,
    integrals, transform, t_hi, t_lo, w_hi, w_lo, amps, part, core_in, x_in, done, back,
    load_sem, amps_send, amps_recv, core_send, core_recv, x_send, x_recv, back_send, back_recv,
):
    me, rep = lax.axis_index("pair"), lax.axis_index("rep")
    hi, lo = lax.div(rep, 2), lax.rem(rep, 2)
    near, far = hi * 2 + (1 - lo), (1 - hi) * 2 + lo
    slabs, rows, width = integrals.shape

    load_own = pltpu.make_async_copy(amps_out.at[0], amps.at[0], load_sem.at[0])
    load_integrals = pltpu.make_async_copy(integrals_in, integrals, load_sem.at[1])
    load_transform = pltpu.make_async_copy(transform_in, transform, load_sem.at[2])
    load_own.start()
    load_transform.start()
    load_integrals.start()

    barrier = pltpu.get_barrier_semaphore()

    @pl.loop(1, n)
    def _(slot):
        other = partner(me, slot, n)
        pl.semaphore_signal(barrier, inc=1, device_id=(other, rep), device_id_type=MESH)

    pl.semaphore_signal(barrier, inc=1, device_id=(me, near), device_id_type=MESH)
    pl.semaphore_signal(barrier, inc=1, device_id=(me, far), device_id_type=MESH)

    def send_amps(slot):
        other = partner(me, slot, n)
        return pltpu.make_async_remote_copy(
            src_ref=amps_out.at[slot], dst_ref=amps.at[slot],
            send_sem=amps_send.at[slot], recv_sem=amps_recv.at[slot],
            device_id=(other, rep), device_id_type=MESH,
        )

    def send_core(slot):
        return pltpu.make_async_remote_copy(
            src_ref=part.at[slot, 1 - lo], dst_ref=core_in.at[slot],
            send_sem=core_send.at[slot], recv_sem=core_recv.at[slot],
            device_id=(me, near), device_id_type=MESH,
        )

    def send_x(slot):
        return pltpu.make_async_remote_copy(
            src_ref=part.at[slot, lo, 1 - hi], dst_ref=x_in.at[slot],
            send_sem=x_send.at[slot], recv_sem=x_recv.at[slot],
            device_id=(me, far), device_id_type=MESH,
        )

    def send_back(slot):
        owner = partner(me, slot, n)
        return pltpu.make_async_remote_copy(
            src_ref=done.at[slot], dst_ref=back.at[slot],
            send_sem=back_send.at[slot], recv_sem=back_recv.at[slot],
            device_id=(owner, rep), device_id_type=MESH,
        )

    pl.semaphore_wait(barrier, n + 1)

    half = n // 2

    @pl.loop(half, half + AHEAD)
    def _(slot):
        send_amps(slot).start()

    @pl.loop(1, half)
    def _(slot):
        send_amps(slot).start()

    load_transform.wait()

    @pl.loop(0, width, step=256)
    def _(k):
        block = transform[pl.ds(k, 256), :]
        high = block.astype(jnp.bfloat16)
        t_hi[pl.ds(k, 256), :] = high
        t_lo[pl.ds(k, 256), :] = (block - high.astype(jnp.float32)).astype(jnp.bfloat16)

    load_integrals.wait()
    for at in range(0, t_hi.shape[1], 2 * LANES):
        flat = integrals[...].reshape(slabs * rows, width)
        columns = slice(at, at + 2 * LANES)
        w = jnp.dot(flat, t_lo[:, columns], preferred_element_type=jnp.float32)
        w += jnp.dot(flat, t_hi[:, columns], preferred_element_type=jnp.float32)
        high = w.astype(jnp.bfloat16)
        w_hi[:, columns] = high
        w_lo[:, columns] = (w - high.astype(jnp.float32)).astype(jnp.bfloat16)

    load_own.wait()

    def multiply(first, last):
        @pl.loop(first, last)
        def _(slot):
            @pl.when(slot >= 1)
            def _():
                send_amps(slot).wait_recv()

            @pl.when(jnp.logical_and(slot >= half, slot < n - AHEAD))
            def _():
                send_amps(slot).wait_send()
                send_amps(slot + AHEAD).start()

            block = amps[slot]
            for h in range(2):
                columns = slice(h * 2 * LANES, (h + 1) * 2 * LANES)
                p = jnp.dot(block, w_lo[:, columns], preferred_element_type=jnp.float32)
                p += jnp.dot(block, w_hi[:, columns], preferred_element_type=jnp.float32)
                part[slot, 0, h] = p[:, :LANES]
                part[slot, 1, h] = p[:, LANES:]
            send_core(slot).start()

    def sum_core(first, last):
        @pl.loop(first, last)
        def _(slot):
            send_core(slot).wait_recv()
            part[slot, lo, 1 - hi] = part[slot, lo, 1 - hi] + core_in[slot, 1 - hi]
            send_x(slot).start()

    def sum_x(first, last):
        @pl.loop(first, last)
        def _(slot):
            send_x(slot).wait_recv()
            done[slot] = part[slot, lo, hi] + core_in[slot, hi] + x_in[slot]

            @pl.when(slot >= 1)
            def _():
                send_back(slot).start()

    groups = [(0, half)] + [(at, min(at + AHEAD, n)) for at in range(half, n, AHEAD)]
    for at, group in enumerate(groups):
        multiply(*group)
        if at:
            sum_x(*groups[at - 1])
        sum_core(*group)
    sum_x(*groups[-1])

    out[...] = done[0]

    @pl.loop(1, n)
    def _(slot):
        send_back(slot).wait_recv()
        out[...] = out[...] + back[slot]

    @pl.loop(0, n)
    def _(slot):
        @pl.when(slot >= 1)
        def _():
            send_back(slot).wait_send()

        @pl.when(jnp.logical_or(jnp.logical_and(slot >= 1, slot < half), slot >= n - AHEAD))
        def _():
            send_amps(slot).wait_send()

        send_core(slot).wait_send()
        send_x(slot).wait_send()


def solution(mesh):
    n, reps = mesh.shape["pair"], mesh.shape["rep"]

    def body(tau_ao, slab_sizes, integrals, transform):
        pairs, packed = tau_ao.shape
        slabs, rows, width = integrals.shape
        virtuals = transform.shape[1]
        assert reps == 4 and rows == LANES and virtuals == reps * LANES
        slots = slabs * rows
        bf, f32, dma = jnp.bfloat16, jnp.float32, pltpu.SemaphoreType.DMA
        flops = 4 * slots * width * virtuals + 4 * n * pairs * slots * virtuals
        amps = pl.pallas_call(
            functools.partial(pick_kernel, n, slabs),
            out_shape=jax.ShapeDtypeStruct((n, pairs, slots), bf),
            in_specs=[pl.BlockSpec(memory_space=pltpu.HBM)] * 2,
            out_specs=pl.BlockSpec(memory_space=pltpu.VMEM),
            scratch_shapes=[pltpu.SMEM((slab_sizes.shape[0],), jnp.int32)] * 2 + [
                pltpu.VMEM((pairs, packed), bf),
                dma((2,)),
            ],
            compiler_params=pltpu.CompilerParams(vmem_limit_bytes=211 << 18),
            cost_estimate=pl.CostEstimate(flops=0, bytes_accessed=2 << 20, transcendentals=0),
        )(slab_sizes, tau_ao)
        return pl.pallas_call(
            functools.partial(kernel, n),
            out_shape=jax.ShapeDtypeStruct((pairs, LANES), f32),
            in_specs=[pl.BlockSpec(memory_space=pltpu.VMEM)] + [pl.BlockSpec(memory_space=pltpu.HBM)] * 2,
            out_specs=pl.BlockSpec(memory_space=pltpu.VMEM),
            scratch_shapes=[
                pltpu.VMEM((slabs, rows, width), bf),
                pltpu.VMEM((width, virtuals), f32),
                pltpu.VMEM((width, virtuals), bf),
                pltpu.VMEM((width, virtuals), bf),
                pltpu.VMEM((slots, virtuals), bf),
                pltpu.VMEM((slots, virtuals), bf),
                pltpu.VMEM((n, pairs, slots), bf),
                pltpu.VMEM((n, 2, 2, pairs, LANES), f32),
                pltpu.VMEM((n, 2, pairs, LANES), f32),
                pltpu.VMEM((n, pairs, LANES), f32),
                pltpu.VMEM((n, pairs, LANES), f32),
                pltpu.VMEM((n, pairs, LANES), f32),
                dma((3,)),
            ] + [dma((n,))] * 8,
            compiler_params=pltpu.CompilerParams(
                collective_id=0, has_side_effects=True, vmem_limit_bytes=211 << 18
            ),
            cost_estimate=pl.CostEstimate(flops=flops, bytes_accessed=4 << 20, transcendentals=0),
        )(amps, integrals, transform)

    return jax.shard_map(
        body,
        mesh=mesh,
        in_specs=(P("pair", None), P(), P("pair", "rep", None), P()),
        out_specs=P("pair", "rep"),
        check_vma=False,
    )
```

```python
import functools

import jax
import jax.numpy as jnp
from jax import lax
from jax.experimental import pallas as pl
from jax.experimental.pallas import tpu as pltpu
from jax.sharding import PartitionSpec as P

MESH = pl.DeviceIdType.MESH
LANES = 128
AHEAD = 3


def partner(me, slot, n):
    other, bit = 0, 1
    while bit < n:
        other += lax.rem(lax.div(me, bit) + lax.div(slot, bit), 2) * bit
        bit *= 2
    return other


def pick_kernel(n, slabs, sizes_in, tau_in, target, offsets, sizes, tau, load_sem):
    me, rep = lax.axis_index("pair"), lax.axis_index("rep")
    pairs, packed = tau.shape
    rows = target.shape[2] // slabs

    load_sizes = pltpu.make_async_copy(sizes_in, sizes, load_sem.at[0])
    load_tau = pltpu.make_async_copy(tau_in, tau, load_sem.at[1])
    load_sizes.start()
    load_tau.start()
    load_sizes.wait()

    def add_up(s, total):
        offsets[s] = total
        return total + sizes[s]

    lax.fori_loop(0, sizes.shape[0], add_up, jnp.int32(0))
    places = lax.broadcasted_iota(jnp.int32, (pairs, rows), 1) + rep * rows
    load_tau.wait()

    @pl.loop(0, n)
    def _(slot):
        dest = partner(me, slot, n)
        for q in range(slabs):
            slab = dest * slabs + q
            start = jnp.minimum(offsets[slab] + rep * rows, packed - 1)
            base = jnp.minimum(lax.div(start, LANES) * LANES, packed - 2 * LANES)
            window = tau[:, pl.ds(pl.multiple_of(base, LANES), 2 * LANES)].astype(jnp.float32)
            turned = pltpu.roll(window, lax.rem(2 * LANES - (start - base), 2 * LANES), 1)[:, :rows]
            kept = jnp.where(places < sizes[slab], turned, 0.0)
            target[slot, :, q * rows : (q + 1) * rows] = kept.astype(jnp.bfloat16)


def kernel(
    n, amps_out, integrals_in, transform_in, out,
    integrals, transform, t_hi, t_lo, w_hi, w_lo, amps, part, core_in, x_in, done, y_in, back,
    load_sem, amps_send, amps_recv, core_send, core_recv, x_send, x_recv, y_send, y_recv, back_send, back_recv,
):
    me, rep = lax.axis_index("pair"), lax.axis_index("rep")
    hi, lo = lax.div(rep, 2), lax.rem(rep, 2)
    near, far = hi * 2 + (1 - lo), (1 - hi) * 2 + lo
    slabs, rows, width = integrals.shape

    load_own = pltpu.make_async_copy(amps_out.at[0], amps.at[0], load_sem.at[0])
    load_integrals = pltpu.make_async_copy(integrals_in, integrals, load_sem.at[1])
    load_transform = pltpu.make_async_copy(transform_in, transform, load_sem.at[2])
    load_own.start()
    load_transform.start()
    load_integrals.start()

    barrier = pltpu.get_barrier_semaphore()

    @pl.loop(1, n)
    def _(slot):
        other = partner(me, slot, n)
        pl.semaphore_signal(barrier, inc=1, device_id=(other, rep), device_id_type=MESH)

    pl.semaphore_signal(barrier, inc=1, device_id=(me, near), device_id_type=MESH)
    pl.semaphore_signal(barrier, inc=1, device_id=(me, far), device_id_type=MESH)

    def send_amps(slot):
        other = partner(me, slot, n)
        return pltpu.make_async_remote_copy(
            src_ref=amps_out.at[slot], dst_ref=amps.at[slot],
            send_sem=amps_send.at[slot], recv_sem=amps_recv.at[slot],
            device_id=(other, rep), device_id_type=MESH,
        )

    def send_core(slot):
        return pltpu.make_async_remote_copy(
            src_ref=part.at[slot, 1 - lo], dst_ref=core_in.at[slot],
            send_sem=core_send.at[slot], recv_sem=core_recv.at[slot],
            device_id=(me, near), device_id_type=MESH,
        )

    def send_x(slot):
        return pltpu.make_async_remote_copy(
            src_ref=part.at[slot, lo, 1 - hi], dst_ref=x_in.at[slot],
            send_sem=x_send.at[slot], recv_sem=x_recv.at[slot],
            device_id=(me, far), device_id_type=MESH,
        )

    def send_y(slot):
        return pltpu.make_async_remote_copy(
            src_ref=done.at[slot], dst_ref=y_in.at[slot],
            send_sem=y_send.at[slot], recv_sem=y_recv.at[slot],
            device_id=(partner(me, 1, n), rep), device_id_type=MESH,
        )

    def send_back(duo):
        return pltpu.make_async_remote_copy(
            src_ref=done.at[2 * duo], dst_ref=back.at[duo],
            send_sem=back_send.at[duo], recv_sem=back_recv.at[duo],
            device_id=(partner(me, 2 * duo, n), rep), device_id_type=MESH,
        )

    pl.semaphore_wait(barrier, n + 1)

    half = n // 2

    @pl.loop(half, half + AHEAD)
    def _(slot):
        send_amps(slot).start()

    @pl.loop(1, half)
    def _(slot):
        send_amps(slot).start()

    load_transform.wait()

    @pl.loop(0, width, step=256)
    def _(k):
        block = transform[pl.ds(k, 256), :]
        high = block.astype(jnp.bfloat16)
        t_hi[pl.ds(k, 256), :] = high
        t_lo[pl.ds(k, 256), :] = (block - high.astype(jnp.float32)).astype(jnp.bfloat16)

    load_integrals.wait()
    for at in range(0, t_hi.shape[1], 2 * LANES):
        flat = integrals[...].reshape(slabs * rows, width)
        columns = slice(at, at + 2 * LANES)
        w = jnp.dot(flat, t_lo[:, columns], preferred_element_type=jnp.float32)
        w += jnp.dot(flat, t_hi[:, columns], preferred_element_type=jnp.float32)
        high = w.astype(jnp.bfloat16)
        w_hi[:, columns] = high
        w_lo[:, columns] = (w - high.astype(jnp.float32)).astype(jnp.bfloat16)

    load_own.wait()

    def multiply(first, last):
        @pl.loop(first, last)
        def _(slot):
            @pl.when(slot >= 1)
            def _():
                send_amps(slot).wait_recv()

            @pl.when(jnp.logical_and(slot >= half, slot < n - AHEAD))
            def _():
                send_amps(slot).wait_send()
                send_amps(slot + AHEAD).start()

            block = amps[slot]
            for h in range(2):
                columns = slice(h * 2 * LANES, (h + 1) * 2 * LANES)
                p = jnp.dot(block, w_lo[:, columns], preferred_element_type=jnp.float32)
                p += jnp.dot(block, w_hi[:, columns], preferred_element_type=jnp.float32)
                part[slot, 0, h] = p[:, :LANES]
                part[slot, 1, h] = p[:, LANES:]
            send_core(slot).start()

    def sum_core(first, last):
        @pl.loop(first, last)
        def _(slot):
            send_core(slot).wait_recv()
            part[slot, lo, 1 - hi] = part[slot, lo, 1 - hi] + core_in[slot, 1 - hi]
            send_x(slot).start()

    def sum_x(first, last):
        @pl.loop(first, last)
        def _(slot):
            send_x(slot).wait_recv()
            done[slot] = part[slot, lo, hi] + core_in[slot, hi] + x_in[slot]

            @pl.when(lax.rem(slot, 2) == 1)
            def _():
                send_y(slot).start()

    def sum_y(first, last):
        @pl.loop(first // 2, last // 2)
        def _(duo):
            send_y(2 * duo + 1).wait_recv()
            done[2 * duo] = done[2 * duo] + y_in[2 * duo + 1]

            @pl.when(duo >= 1)
            def _():
                send_back(duo).start()

    groups = [(0, half)] + [(at, min(at + AHEAD, n)) for at in range(half, n, AHEAD)]
    for at, group in enumerate(groups):
        multiply(*group)
        if at:
            sum_x(*groups[at - 1])
        sum_core(*group)
        if at:
            sum_y(*groups[at - 1])
    sum_x(*groups[-1])
    sum_y(*groups[-1])

    out[...] = done[0]

    @pl.loop(1, half)
    def _(duo):
        send_back(duo).wait_recv()
        out[...] = out[...] + back[duo]

    @pl.loop(0, n)
    def _(slot):
        @pl.when(jnp.logical_or(jnp.logical_and(slot >= 1, slot < half), slot >= n - AHEAD))
        def _():
            send_amps(slot).wait_send()

        @pl.when(lax.rem(slot, 2) == 1)
        def _():
            send_y(slot).wait_send()

        send_core(slot).wait_send()
        send_x(slot).wait_send()

    @pl.loop(1, half)
    def _(duo):
        send_back(duo).wait_send()


def solution(mesh):
    n, reps = mesh.shape["pair"], mesh.shape["rep"]

    def body(tau_ao, slab_sizes, integrals, transform):
        pairs, packed = tau_ao.shape
        slabs, rows, width = integrals.shape
        virtuals = transform.shape[1]
        assert reps == 4 and rows == LANES and virtuals == reps * LANES
        slots = slabs * rows
        bf, f32, dma = jnp.bfloat16, jnp.float32, pltpu.SemaphoreType.DMA
        flops = 4 * slots * width * virtuals + 4 * n * pairs * slots * virtuals
        amps = pl.pallas_call(
            functools.partial(pick_kernel, n, slabs),
            out_shape=jax.ShapeDtypeStruct((n, pairs, slots), bf),
            in_specs=[pl.BlockSpec(memory_space=pltpu.HBM)] * 2,
            out_specs=pl.BlockSpec(memory_space=pltpu.VMEM),
            scratch_shapes=[pltpu.SMEM((slab_sizes.shape[0],), jnp.int32)] * 2 + [
                pltpu.VMEM((pairs, packed), bf),
                dma((2,)),
            ],
            compiler_params=pltpu.CompilerParams(vmem_limit_bytes=211 << 18),
            cost_estimate=pl.CostEstimate(flops=0, bytes_accessed=2 << 20, transcendentals=0),
        )(slab_sizes, tau_ao)
        return pl.pallas_call(
            functools.partial(kernel, n),
            out_shape=jax.ShapeDtypeStruct((pairs, LANES), f32),
            in_specs=[pl.BlockSpec(memory_space=pltpu.VMEM)] + [pl.BlockSpec(memory_space=pltpu.HBM)] * 2,
            out_specs=pl.BlockSpec(memory_space=pltpu.VMEM),
            scratch_shapes=[
                pltpu.VMEM((slabs, rows, width), bf),
                pltpu.VMEM((width, virtuals), f32),
                pltpu.VMEM((width, virtuals), bf),
                pltpu.VMEM((width, virtuals), bf),
                pltpu.VMEM((slots, virtuals), bf),
                pltpu.VMEM((slots, virtuals), bf),
                pltpu.VMEM((n, pairs, slots), bf),
                pltpu.VMEM((n, 2, 2, pairs, LANES), f32),
                pltpu.VMEM((n, 2, pairs, LANES), f32),
                pltpu.VMEM((n, pairs, LANES), f32),
                pltpu.VMEM((n, pairs, LANES), f32),
                pltpu.VMEM((n, pairs, LANES), f32),
                pltpu.VMEM((n // 2, pairs, LANES), f32),
                dma((3,)),
            ] + [dma((n,))] * 8 + [dma((n // 2,))] * 2,
            compiler_params=pltpu.CompilerParams(
                collective_id=0, has_side_effects=True, vmem_limit_bytes=211 << 18
            ),
            cost_estimate=pl.CostEstimate(flops=flops, bytes_accessed=4 << 20, transcendentals=0),
        )(amps, integrals, transform)

    return jax.shard_map(
        body,
        mesh=mesh,
        in_specs=(P("pair", None), P(), P("pair", "rep", None), P()),
        out_specs=P("pair", "rep"),
        check_vma=False,
    )
```

```python
import functools

import jax
import jax.numpy as jnp
from jax import lax
from jax.experimental import pallas as pl
from jax.experimental.pallas import tpu as pltpu
from jax.sharding import PartitionSpec as P

MESH = pl.DeviceIdType.MESH
LANES = 128
AHEAD = 3


def partner(me, slot, n):
    other, bit = 0, 1
    while bit < n:
        other += lax.rem(lax.div(me, bit) + lax.div(slot, bit), 2) * bit
        bit *= 2
    return other


def pick_kernel(n, slabs, sizes_in, tau_in, target, offsets, sizes, tau, load_sem):
    me, rep = lax.axis_index("pair"), lax.axis_index("rep")
    pairs, packed = tau.shape
    rows = target.shape[2] // slabs

    load_sizes = pltpu.make_async_copy(sizes_in, sizes, load_sem.at[0])
    load_tau = pltpu.make_async_copy(tau_in, tau, load_sem.at[1])
    load_sizes.start()
    load_tau.start()
    load_sizes.wait()

    def add_up(s, total):
        offsets[s] = total
        return total + sizes[s]

    lax.fori_loop(0, sizes.shape[0], add_up, jnp.int32(0))
    places = lax.broadcasted_iota(jnp.int32, (pairs, rows), 1) + rep * rows
    load_tau.wait()

    @pl.loop(0, n)
    def _(slot):
        dest = partner(me, slot, n)
        for q in range(slabs):
            slab = dest * slabs + q
            start = jnp.minimum(offsets[slab] + rep * rows, packed - 1)
            base = jnp.minimum(lax.div(start, LANES) * LANES, packed - 2 * LANES)
            window = tau[:, pl.ds(pl.multiple_of(base, LANES), 2 * LANES)].astype(jnp.float32)
            turned = pltpu.roll(window, lax.rem(2 * LANES - (start - base), 2 * LANES), 1)[:, :rows]
            kept = jnp.where(places < sizes[slab], turned, 0.0)
            target[slot, :, q * rows : (q + 1) * rows] = kept.astype(jnp.bfloat16)


def kernel(
    n, reps, groups, amps_out, integrals_in, transform_in, out,
    integrals, transform, t_hi, t_lo, w_hi, w_lo, amps, part, rep_in, done, back,
    load_sem, amps_send, amps_recv, rep_send, rep_recv, back_send, back_recv,
):
    me, rep = lax.axis_index("pair"), lax.axis_index("rep")
    slabs, rows, width = integrals.shape

    load_own = pltpu.make_async_copy(amps_out.at[0], amps.at[0], load_sem.at[0])
    load_integrals = pltpu.make_async_copy(integrals_in, integrals, load_sem.at[1])
    load_transform = pltpu.make_async_copy(transform_in, transform, load_sem.at[2])
    load_own.start()
    load_transform.start()
    load_integrals.start()

    barrier = pltpu.get_barrier_semaphore()

    @pl.loop(1, n)
    def _(slot):
        other = partner(me, slot, n)
        pl.semaphore_signal(barrier, inc=1, device_id=(other, rep), device_id_type=MESH)

    for d in range(1, reps):
        pl.semaphore_signal(barrier, inc=1, device_id=(me, partner(rep, d, reps)), device_id_type=MESH)

    def send_amps(slot):
        other = partner(me, slot, n)
        return pltpu.make_async_remote_copy(
            src_ref=amps_out.at[slot], dst_ref=amps.at[slot],
            send_sem=amps_send.at[slot], recv_sem=amps_recv.at[slot],
            device_id=(other, rep), device_id_type=MESH,
        )

    def send_rep(d, at):
        first, last = groups[at]
        held = pl.ds(first, last - first)
        other = partner(rep, d, reps)
        return pltpu.make_async_remote_copy(
            src_ref=part.at[other, held], dst_ref=rep_in.at[d - 1, held],
            send_sem=rep_send.at[d - 1, at], recv_sem=rep_recv.at[d - 1, at],
            device_id=(me, other), device_id_type=MESH,
        )

    def send_back(slot):
        owner = partner(me, slot, n)
        return pltpu.make_async_remote_copy(
            src_ref=done.at[slot], dst_ref=back.at[slot],
            send_sem=back_send.at[slot], recv_sem=back_recv.at[slot],
            device_id=(owner, rep), device_id_type=MESH,
        )

    pl.semaphore_wait(barrier, n + reps - 2)

    half = n // 2

    @pl.loop(half, half + AHEAD)
    def _(slot):
        send_amps(slot).start()

    @pl.loop(1, half)
    def _(slot):
        send_amps(slot).start()

    load_transform.wait()

    @pl.loop(0, width, step=256)
    def _(k):
        block = transform[pl.ds(k, 256), :]
        high = block.astype(jnp.bfloat16)
        t_hi[pl.ds(k, 256), :] = high
        t_lo[pl.ds(k, 256), :] = (block - high.astype(jnp.float32)).astype(jnp.bfloat16)

    load_integrals.wait()
    for at in range(0, t_hi.shape[1], 2 * LANES):
        flat = integrals[...].reshape(slabs * rows, width)
        columns = slice(at, at + 2 * LANES)
        w = jnp.dot(flat, t_lo[:, columns], preferred_element_type=jnp.float32)
        w += jnp.dot(flat, t_hi[:, columns], preferred_element_type=jnp.float32)
        high = w.astype(jnp.bfloat16)
        w_hi[:, columns] = high
        w_lo[:, columns] = (w - high.astype(jnp.float32)).astype(jnp.bfloat16)

    load_own.wait()

    def multiply(first, last):
        @pl.loop(first, last)
        def _(slot):
            @pl.when(slot >= 1)
            def _():
                send_amps(slot).wait_recv()

            @pl.when(jnp.logical_and(slot >= half, slot < n - AHEAD))
            def _():
                send_amps(slot).wait_send()
                send_amps(slot + AHEAD).start()

            block = amps[slot]
            for h in range(2):
                columns = slice(h * 2 * LANES, (h + 1) * 2 * LANES)
                p = jnp.dot(block, w_lo[:, columns], preferred_element_type=jnp.float32)
                p += jnp.dot(block, w_hi[:, columns], preferred_element_type=jnp.float32)
                part[2 * h, slot] = p[:, :LANES]
                part[2 * h + 1, slot] = p[:, LANES:]

    def sum_rep(first, last):
        @pl.loop(first, last)
        def _(slot):
            total = part[rep, slot]
            for d in range(1, reps):
                total = total + rep_in[d - 1, slot]
            done[slot] = total

            @pl.when(slot >= 1)
            def _():
                send_back(slot).start()

    for at in range(len(groups) + 1):
        if at < len(groups):
            multiply(*groups[at])
            for d in range(1, reps):
                send_rep(d, at).start()
        if at:
            for d in range(1, reps):
                send_rep(d, at - 1).wait_recv()
            sum_rep(*groups[at - 1])

    out[...] = done[0]

    @pl.loop(1, n)
    def _(slot):
        send_back(slot).wait_recv()
        out[...] = out[...] + back[slot]

    @pl.loop(0, n)
    def _(slot):
        @pl.when(slot >= 1)
        def _():
            send_back(slot).wait_send()

        @pl.when(jnp.logical_or(jnp.logical_and(slot >= 1, slot < half), slot >= n - AHEAD))
        def _():
            send_amps(slot).wait_send()

    for at in range(len(groups)):
        for d in range(1, reps):
            send_rep(d, at).wait_send()


def solution(mesh):
    n, reps = mesh.shape["pair"], mesh.shape["rep"]

    def body(tau_ao, slab_sizes, integrals, transform):
        pairs, packed = tau_ao.shape
        slabs, rows, width = integrals.shape
        virtuals = transform.shape[1]
        assert reps == 4 and rows == LANES and virtuals == reps * LANES
        slots = slabs * rows
        half = n // 2
        groups = [(0, half)] + [(at, min(at + AHEAD, n)) for at in range(half, n, AHEAD)]
        bf, f32, dma = jnp.bfloat16, jnp.float32, pltpu.SemaphoreType.DMA
        flops = 4 * slots * width * virtuals + 4 * n * pairs * slots * virtuals
        amps = pl.pallas_call(
            functools.partial(pick_kernel, n, slabs),
            out_shape=jax.ShapeDtypeStruct((n, pairs, slots), bf),
            in_specs=[pl.BlockSpec(memory_space=pltpu.HBM)] * 2,
            out_specs=pl.BlockSpec(memory_space=pltpu.VMEM),
            scratch_shapes=[pltpu.SMEM((slab_sizes.shape[0],), jnp.int32)] * 2 + [
                pltpu.VMEM((pairs, packed), bf),
                dma((2,)),
            ],
            compiler_params=pltpu.CompilerParams(vmem_limit_bytes=211 << 18),
            cost_estimate=pl.CostEstimate(flops=0, bytes_accessed=2 << 20, transcendentals=0),
        )(slab_sizes, tau_ao)
        return pl.pallas_call(
            functools.partial(kernel, n, reps, groups),
            out_shape=jax.ShapeDtypeStruct((pairs, LANES), f32),
            in_specs=[pl.BlockSpec(memory_space=pltpu.VMEM)] + [pl.BlockSpec(memory_space=pltpu.HBM)] * 2,
            out_specs=pl.BlockSpec(memory_space=pltpu.VMEM),
            scratch_shapes=[
                pltpu.VMEM((slabs, rows, width), bf),
                pltpu.VMEM((width, virtuals), f32),
                pltpu.VMEM((width, virtuals), bf),
                pltpu.VMEM((width, virtuals), bf),
                pltpu.VMEM((slots, virtuals), bf),
                pltpu.VMEM((slots, virtuals), bf),
                pltpu.VMEM((n, pairs, slots), bf),
                pltpu.VMEM((reps, n, pairs, LANES), f32),
                pltpu.VMEM((reps - 1, n, pairs, LANES), f32),
                pltpu.VMEM((n, pairs, LANES), f32),
                pltpu.VMEM((n, pairs, LANES), f32),
                dma((3,)),
            ] + [dma((n,))] * 2 + [dma((reps - 1, len(groups)))] * 2 + [dma((n,))] * 2,
            compiler_params=pltpu.CompilerParams(
                collective_id=0, has_side_effects=True, vmem_limit_bytes=211 << 18
            ),
            cost_estimate=pl.CostEstimate(flops=flops, bytes_accessed=4 << 20, transcendentals=0),
        )(amps, integrals, transform)

    return jax.shard_map(
        body,
        mesh=mesh,
        in_specs=(P("pair", None), P(), P("pair", "rep", None), P()),
        out_specs=P("pair", "rep"),
        check_vma=False,
    )
```

```python
import functools

import jax
import jax.numpy as jnp
from jax import lax
from jax.experimental import pallas as pl
from jax.experimental.pallas import tpu as pltpu
from jax.sharding import PartitionSpec as P

MESH = pl.DeviceIdType.MESH
LANES = 128
AHEAD = 3


def partner(me, slot, n):
    other, bit = 0, 1
    while bit < n:
        other += lax.rem(lax.div(me, bit) + lax.div(slot, bit), 2) * bit
        bit *= 2
    return other


def pick_kernel(n, slabs, sizes_in, tau_in, target, offsets, sizes, tau, load_sem):
    me, rep = lax.axis_index("pair"), lax.axis_index("rep")
    pairs, packed = tau.shape
    rows = target.shape[2] // slabs

    load_sizes = pltpu.make_async_copy(sizes_in, sizes, load_sem.at[0])
    load_tau = pltpu.make_async_copy(tau_in, tau, load_sem.at[1])
    load_sizes.start()
    load_tau.start()
    load_sizes.wait()

    def add_up(s, total):
        offsets[s] = total
        return total + sizes[s]

    lax.fori_loop(0, sizes.shape[0], add_up, jnp.int32(0))
    places = lax.broadcasted_iota(jnp.int32, (pairs, rows), 1) + rep * rows
    load_tau.wait()

    @pl.loop(0, n)
    def _(slot):
        dest = partner(me, slot, n)
        for q in range(slabs):
            slab = dest * slabs + q
            start = jnp.minimum(offsets[slab] + rep * rows, packed - 1)
            base = jnp.minimum(lax.div(start, LANES) * LANES, packed - 2 * LANES)
            window = tau[:, pl.ds(pl.multiple_of(base, LANES), 2 * LANES)].astype(jnp.float32)
            turned = pltpu.roll(window, lax.rem(2 * LANES - (start - base), 2 * LANES), 1)[:, :rows]
            kept = jnp.where(places < sizes[slab], turned, 0.0)
            target[slot, :, q * rows : (q + 1) * rows] = kept.astype(jnp.bfloat16)


def kernel(
    n, groups, amps_out, integrals_in, transform_in, out,
    integrals, transform, t_hi, t_lo, w_hi, w_lo, amps, part, core_in, x_in, rep_in, done, back,
    load_sem, amps_send, amps_recv, core_send, core_recv, x_send, x_recv, rep_send, rep_recv, back_send, back_recv,
):
    me, rep = lax.axis_index("pair"), lax.axis_index("rep")
    hi, lo = lax.div(rep, 2), lax.rem(rep, 2)
    near, far = hi * 2 + (1 - lo), (1 - hi) * 2 + lo
    both = (1 - hi) * 2 + (1 - lo)
    slabs, rows, width = integrals.shape

    load_own = pltpu.make_async_copy(amps_out.at[0], amps.at[0], load_sem.at[0])
    load_integrals = pltpu.make_async_copy(integrals_in, integrals, load_sem.at[1])
    load_transform = pltpu.make_async_copy(transform_in, transform, load_sem.at[2])
    load_own.start()
    load_transform.start()
    load_integrals.start()

    barrier = pltpu.get_barrier_semaphore()

    @pl.loop(1, n)
    def _(slot):
        other = partner(me, slot, n)
        pl.semaphore_signal(barrier, inc=1, device_id=(other, rep), device_id_type=MESH)

    pl.semaphore_signal(barrier, inc=1, device_id=(me, near), device_id_type=MESH)
    pl.semaphore_signal(barrier, inc=1, device_id=(me, far), device_id_type=MESH)
    pl.semaphore_signal(barrier, inc=1, device_id=(me, both), device_id_type=MESH)

    def send_amps(slot):
        other = partner(me, slot, n)
        return pltpu.make_async_remote_copy(
            src_ref=amps_out.at[slot], dst_ref=amps.at[slot],
            send_sem=amps_send.at[slot], recv_sem=amps_recv.at[slot],
            device_id=(other, rep), device_id_type=MESH,
        )

    def send_core(slot):
        return pltpu.make_async_remote_copy(
            src_ref=part.at[slot, 1 - lo], dst_ref=core_in.at[slot],
            send_sem=core_send.at[slot], recv_sem=core_recv.at[slot],
            device_id=(me, near), device_id_type=MESH,
        )

    def send_x(slot):
        return pltpu.make_async_remote_copy(
            src_ref=part.at[slot, lo, 1 - hi], dst_ref=x_in.at[slot],
            send_sem=x_send.at[slot], recv_sem=x_recv.at[slot],
            device_id=(me, far), device_id_type=MESH,
        )

    def send_direct(slot, way):
        other = (near, far, both)[way]
        at = slot - groups[-1][0]
        return pltpu.make_async_remote_copy(
            src_ref=part.at[slot, lax.rem(other, 2), lax.div(other, 2)], dst_ref=rep_in.at[at, way],
            send_sem=rep_send.at[at, way], recv_sem=rep_recv.at[at, way],
            device_id=(me, other), device_id_type=MESH,
        )

    def send_back(slot):
        owner = partner(me, slot, n)
        return pltpu.make_async_remote_copy(
            src_ref=done.at[slot], dst_ref=back.at[slot],
            send_sem=back_send.at[slot], recv_sem=back_recv.at[slot],
            device_id=(owner, rep), device_id_type=MESH,
        )

    pl.semaphore_wait(barrier, n + 2)

    half = n // 2

    @pl.loop(half, half + AHEAD)
    def _(slot):
        send_amps(slot).start()

    @pl.loop(1, half)
    def _(slot):
        send_amps(slot).start()

    load_transform.wait()

    @pl.loop(0, width, step=256)
    def _(k):
        block = transform[pl.ds(k, 256), :]
        high = block.astype(jnp.bfloat16)
        t_hi[pl.ds(k, 256), :] = high
        t_lo[pl.ds(k, 256), :] = (block - high.astype(jnp.float32)).astype(jnp.bfloat16)

    load_integrals.wait()
    for at in range(0, t_hi.shape[1], 2 * LANES):
        flat = integrals[...].reshape(slabs * rows, width)
        columns = slice(at, at + 2 * LANES)
        w = jnp.dot(flat, t_lo[:, columns], preferred_element_type=jnp.float32)
        w += jnp.dot(flat, t_hi[:, columns], preferred_element_type=jnp.float32)
        high = w.astype(jnp.bfloat16)
        w_hi[:, columns] = high
        w_lo[:, columns] = (w - high.astype(jnp.float32)).astype(jnp.bfloat16)

    load_own.wait()

    def multiply(first, last, direct):
        @pl.loop(first, last)
        def _(slot):
            @pl.when(slot >= 1)
            def _():
                send_amps(slot).wait_recv()

            @pl.when(jnp.logical_and(slot >= half, slot < n - AHEAD))
            def _():
                send_amps(slot).wait_send()
                send_amps(slot + AHEAD).start()

            block = amps[slot]
            for h in range(2):
                columns = slice(h * 2 * LANES, (h + 1) * 2 * LANES)
                p = jnp.dot(block, w_lo[:, columns], preferred_element_type=jnp.float32)
                p += jnp.dot(block, w_hi[:, columns], preferred_element_type=jnp.float32)
                part[slot, 0, h] = p[:, :LANES]
                part[slot, 1, h] = p[:, LANES:]
            if direct:
                for way in (1, 2, 0):
                    send_direct(slot, way).start()
            else:
                send_core(slot).start()

    def sum_core(first, last):
        @pl.loop(first, last)
        def _(slot):
            send_core(slot).wait_recv()
            part[slot, lo, 1 - hi] = part[slot, lo, 1 - hi] + core_in[slot, 1 - hi]
            send_x(slot).start()

    def sum_x(first, last):
        @pl.loop(first, last)
        def _(slot):
            send_x(slot).wait_recv()
            done[slot] = part[slot, lo, hi] + core_in[slot, hi] + x_in[slot]

            @pl.when(slot >= 1)
            def _():
                send_back(slot).start()

    def sum_direct(first, last):
        @pl.loop(first, last)
        def _(slot):
            total = part[slot, lo, hi]
            for way in range(3):
                send_direct(slot, way).wait_recv()
                total = total + rep_in[slot - first, way]
            done[slot] = total
            send_back(slot).start()

    for at, group in enumerate(groups):
        direct = at == len(groups) - 1
        multiply(*group, direct)
        if at:
            sum_x(*groups[at - 1])
        if not direct:
            sum_core(*group)
    sum_direct(*groups[-1])

    out[...] = done[0]

    @pl.loop(1, n)
    def _(slot):
        send_back(slot).wait_recv()
        out[...] = out[...] + back[slot]

    @pl.loop(0, n)
    def _(slot):
        @pl.when(slot >= 1)
        def _():
            send_back(slot).wait_send()

        @pl.when(jnp.logical_or(jnp.logical_and(slot >= 1, slot < half), slot >= n - AHEAD))
        def _():
            send_amps(slot).wait_send()

        @pl.when(slot < groups[-1][0])
        def _():
            send_core(slot).wait_send()
            send_x(slot).wait_send()

        @pl.when(slot >= groups[-1][0])
        def _():
            for way in range(3):
                send_direct(slot, way).wait_send()


def solution(mesh):
    n, reps = mesh.shape["pair"], mesh.shape["rep"]

    def body(tau_ao, slab_sizes, integrals, transform):
        pairs, packed = tau_ao.shape
        slabs, rows, width = integrals.shape
        virtuals = transform.shape[1]
        assert reps == 4 and rows == LANES and virtuals == reps * LANES
        slots = slabs * rows
        half = n // 2
        groups = [(0, half)] + [(at, min(at + AHEAD, n)) for at in range(half, n, AHEAD)]
        ending = groups[-1][1] - groups[-1][0]
        bf, f32, dma = jnp.bfloat16, jnp.float32, pltpu.SemaphoreType.DMA
        flops = 4 * slots * width * virtuals + 4 * n * pairs * slots * virtuals
        amps = pl.pallas_call(
            functools.partial(pick_kernel, n, slabs),
            out_shape=jax.ShapeDtypeStruct((n, pairs, slots), bf),
            in_specs=[pl.BlockSpec(memory_space=pltpu.HBM)] * 2,
            out_specs=pl.BlockSpec(memory_space=pltpu.VMEM),
            scratch_shapes=[pltpu.SMEM((slab_sizes.shape[0],), jnp.int32)] * 2 + [
                pltpu.VMEM((pairs, packed), bf),
                dma((2,)),
            ],
            compiler_params=pltpu.CompilerParams(vmem_limit_bytes=211 << 18),
            cost_estimate=pl.CostEstimate(flops=0, bytes_accessed=2 << 20, transcendentals=0),
        )(slab_sizes, tau_ao)
        return pl.pallas_call(
            functools.partial(kernel, n, groups),
            out_shape=jax.ShapeDtypeStruct((pairs, LANES), f32),
            in_specs=[pl.BlockSpec(memory_space=pltpu.VMEM)] + [pl.BlockSpec(memory_space=pltpu.HBM)] * 2,
            out_specs=pl.BlockSpec(memory_space=pltpu.VMEM),
            scratch_shapes=[
                pltpu.VMEM((slabs, rows, width), bf),
                pltpu.VMEM((width, virtuals), f32),
                pltpu.VMEM((width, virtuals), bf),
                pltpu.VMEM((width, virtuals), bf),
                pltpu.VMEM((slots, virtuals), bf),
                pltpu.VMEM((slots, virtuals), bf),
                pltpu.VMEM((n, pairs, slots), bf),
                pltpu.VMEM((n, 2, 2, pairs, LANES), f32),
                pltpu.VMEM((n, 2, pairs, LANES), f32),
                pltpu.VMEM((n, pairs, LANES), f32),
                pltpu.VMEM((ending, 3, pairs, LANES), f32),
                pltpu.VMEM((n, pairs, LANES), f32),
                pltpu.VMEM((n, pairs, LANES), f32),
                dma((3,)),
            ] + [dma((n,))] * 6 + [dma((ending, 3))] * 2 + [dma((n,))] * 2,
            compiler_params=pltpu.CompilerParams(
                collective_id=0, has_side_effects=True, vmem_limit_bytes=211 << 18
            ),
            cost_estimate=pl.CostEstimate(flops=flops, bytes_accessed=4 << 20, transcendentals=0),
        )(amps, integrals, transform)

    return jax.shard_map(
        body,
        mesh=mesh,
        in_specs=(P("pair", None), P(), P("pair", "rep", None), P()),
        out_specs=P("pair", "rep"),
        check_vma=False,
    )
```

```python
import functools

import jax
import jax.numpy as jnp
from jax import lax
from jax.experimental import pallas as pl
from jax.experimental.pallas import tpu as pltpu
from jax.sharding import PartitionSpec as P

MESH = pl.DeviceIdType.MESH
LANES = 128
AHEAD = 3


def partner(me, slot, n):
    other, bit = 0, 1
    while bit < n:
        other += lax.rem(lax.div(me, bit) + lax.div(slot, bit), 2) * bit
        bit *= 2
    return other


def pick_kernel(n, slabs, sizes_in, tau_in, target, offsets, sizes, tau, load_sem):
    me, rep = lax.axis_index("pair"), lax.axis_index("rep")
    pairs, packed = tau.shape
    rows = target.shape[2] // slabs

    load_sizes = pltpu.make_async_copy(sizes_in, sizes, load_sem.at[0])
    load_tau = pltpu.make_async_copy(tau_in, tau, load_sem.at[1])
    load_sizes.start()
    load_tau.start()
    load_sizes.wait()

    def add_up(s, total):
        offsets[s] = total
        return total + sizes[s]

    lax.fori_loop(0, sizes.shape[0], add_up, jnp.int32(0))
    places = lax.broadcasted_iota(jnp.int32, (pairs, rows), 1) + rep * rows
    load_tau.wait()

    @pl.loop(0, n)
    def _(slot):
        dest = partner(me, slot, n)
        for q in range(slabs):
            slab = dest * slabs + q
            start = jnp.minimum(offsets[slab] + rep * rows, packed - 1)
            base = jnp.minimum(lax.div(start, LANES) * LANES, packed - 2 * LANES)
            window = tau[:, pl.ds(pl.multiple_of(base, LANES), 2 * LANES)].astype(jnp.float32)
            turned = pltpu.roll(window, lax.rem(2 * LANES - (start - base), 2 * LANES), 1)[:, :rows]
            kept = jnp.where(places < sizes[slab], turned, 0.0)
            target[slot, :, q * rows : (q + 1) * rows] = kept.astype(jnp.bfloat16)


def kernel(
    n, groups, amps_out, integrals_in, transform_in, out,
    integrals, transform, t_hi, t_lo, w_hi, w_lo, amps, part, core_in, x_in, rep_in, done, back,
    load_sem, amps_send, amps_recv, core_send, core_recv, x_send, x_recv, rep_send, rep_recv, back_send, back_recv,
):
    me, rep = lax.axis_index("pair"), lax.axis_index("rep")
    hi, lo = lax.div(rep, 2), lax.rem(rep, 2)
    near, far = hi * 2 + (1 - lo), (1 - hi) * 2 + lo
    both = (1 - hi) * 2 + (1 - lo)
    slabs, rows, width = integrals.shape

    load_own = pltpu.make_async_copy(amps_out.at[0], amps.at[0], load_sem.at[0])
    load_integrals = pltpu.make_async_copy(integrals_in, integrals, load_sem.at[1])
    load_transform = pltpu.make_async_copy(transform_in, transform, load_sem.at[2])
    load_own.start()
    load_transform.start()
    load_integrals.start()

    barrier = pltpu.get_barrier_semaphore()

    @pl.loop(1, n)
    def _(slot):
        other = partner(me, slot, n)
        pl.semaphore_signal(barrier, inc=1, device_id=(other, rep), device_id_type=MESH)

    pl.semaphore_signal(barrier, inc=1, device_id=(me, near), device_id_type=MESH)
    pl.semaphore_signal(barrier, inc=1, device_id=(me, far), device_id_type=MESH)
    pl.semaphore_signal(barrier, inc=1, device_id=(me, both), device_id_type=MESH)

    def send_amps(slot):
        other = partner(me, slot, n)
        return pltpu.make_async_remote_copy(
            src_ref=amps_out.at[slot], dst_ref=amps.at[slot],
            send_sem=amps_send.at[slot], recv_sem=amps_recv.at[slot],
            device_id=(other, rep), device_id_type=MESH,
        )

    def send_core(slot):
        return pltpu.make_async_remote_copy(
            src_ref=part.at[slot, 1 - lo], dst_ref=core_in.at[slot],
            send_sem=core_send.at[slot], recv_sem=core_recv.at[slot],
            device_id=(me, near), device_id_type=MESH,
        )

    def send_x(slot):
        return pltpu.make_async_remote_copy(
            src_ref=part.at[slot, lo, 1 - hi], dst_ref=x_in.at[slot],
            send_sem=x_send.at[slot], recv_sem=x_recv.at[slot],
            device_id=(me, far), device_id_type=MESH,
        )

    def send_direct(slot, way):
        other = (near, far, both)[way]
        at = slot - groups[-1][0]
        return pltpu.make_async_remote_copy(
            src_ref=part.at[slot, lax.rem(other, 2), lax.div(other, 2)], dst_ref=rep_in.at[at, way],
            send_sem=rep_send.at[at, way], recv_sem=rep_recv.at[at, way],
            device_id=(me, other), device_id_type=MESH,
        )

    def send_back(slot):
        owner = partner(me, slot, n)
        return pltpu.make_async_remote_copy(
            src_ref=done.at[slot], dst_ref=back.at[slot],
            send_sem=back_send.at[slot], recv_sem=back_recv.at[slot],
            device_id=(owner, rep), device_id_type=MESH,
        )

    pl.semaphore_wait(barrier, n + 2)

    half = n // 2

    @pl.loop(half, half + AHEAD)
    def _(slot):
        send_amps(slot).start()

    @pl.loop(1, half)
    def _(slot):
        send_amps(slot).start()

    load_transform.wait()

    @pl.loop(0, width, step=256)
    def _(k):
        block = transform[pl.ds(k, 256), :]
        high = block.astype(jnp.bfloat16)
        t_hi[pl.ds(k, 256), :] = high
        t_lo[pl.ds(k, 256), :] = (block - high.astype(jnp.float32)).astype(jnp.bfloat16)

    load_integrals.wait()
    for at in range(0, t_hi.shape[1], 2 * LANES):
        flat = integrals[...].reshape(slabs * rows, width)
        columns = slice(at, at + 2 * LANES)
        w = jnp.dot(flat, t_lo[:, columns], preferred_element_type=jnp.float32)
        w += jnp.dot(flat, t_hi[:, columns], preferred_element_type=jnp.float32)
        high = w.astype(jnp.bfloat16)
        w_hi[:, columns] = high
        w_lo[:, columns] = (w - high.astype(jnp.float32)).astype(jnp.bfloat16)

    load_own.wait()

    def multiply(first, last, direct):
        @pl.loop(first, last)
        def _(slot):
            @pl.when(slot >= 1)
            def _():
                send_amps(slot).wait_recv()

            @pl.when(jnp.logical_and(slot >= half, slot < n - AHEAD))
            def _():
                send_amps(slot).wait_send()
                send_amps(slot + AHEAD).start()

            block = amps[slot]
            for h in range(2):
                columns = slice(h * 2 * LANES, (h + 1) * 2 * LANES)
                p = jnp.dot(block, w_lo[:, columns], preferred_element_type=jnp.float32)
                p += jnp.dot(block, w_hi[:, columns], preferred_element_type=jnp.float32)
                part[slot, 0, h] = p[:, :LANES]
                part[slot, 1, h] = p[:, LANES:]
            if direct:
                for way in (1, 2, 0):
                    send_direct(slot, way).start()
            else:
                send_core(slot).start()

    def sum_core(first, last):
        @pl.loop(first, last)
        def _(slot):
            send_core(slot).wait_recv()
            part[slot, lo, 1 - hi] = part[slot, lo, 1 - hi] + core_in[slot, 1 - hi]
            send_x(slot).start()

    def sum_x(first, last):
        @pl.loop(first, last)
        def _(slot):
            send_x(slot).wait_recv()
            done[slot] = part[slot, lo, hi] + core_in[slot, hi] + x_in[slot]

            @pl.when(slot >= 1)
            def _():
                send_back(slot).start()

    def sum_direct(first, last):
        @pl.loop(first, last)
        def _(slot):
            total = part[slot, lo, hi]
            for way in range(3):
                send_direct(slot, way).wait_recv()
                total = total + rep_in[slot - first, way]
            done[slot] = total
            send_back(slot).start()

    for at, group in enumerate(groups):
        direct = at == len(groups) - 1
        if direct:
            sum_x(*groups[at - 1])
        multiply(*group, direct)
        if not direct:
            if at:
                sum_x(*groups[at - 1])
            sum_core(*group)
    sum_direct(*groups[-1])

    out[...] = done[0]

    @pl.loop(1, n)
    def _(slot):
        send_back(slot).wait_recv()
        out[...] = out[...] + back[slot]

    @pl.loop(0, n)
    def _(slot):
        @pl.when(slot >= 1)
        def _():
            send_back(slot).wait_send()

        @pl.when(jnp.logical_or(jnp.logical_and(slot >= 1, slot < half), slot >= n - AHEAD))
        def _():
            send_amps(slot).wait_send()

        @pl.when(slot < groups[-1][0])
        def _():
            send_core(slot).wait_send()
            send_x(slot).wait_send()

        @pl.when(slot >= groups[-1][0])
        def _():
            for way in range(3):
                send_direct(slot, way).wait_send()


def solution(mesh):
    n, reps = mesh.shape["pair"], mesh.shape["rep"]

    def body(tau_ao, slab_sizes, integrals, transform):
        pairs, packed = tau_ao.shape
        slabs, rows, width = integrals.shape
        virtuals = transform.shape[1]
        assert reps == 4 and rows == LANES and virtuals == reps * LANES
        slots = slabs * rows
        half = n // 2
        groups = [(0, half)] + [(at, min(at + AHEAD, n)) for at in range(half, n, AHEAD)]
        ending = groups[-1][1] - groups[-1][0]
        bf, f32, dma = jnp.bfloat16, jnp.float32, pltpu.SemaphoreType.DMA
        flops = 4 * slots * width * virtuals + 4 * n * pairs * slots * virtuals
        amps = pl.pallas_call(
            functools.partial(pick_kernel, n, slabs),
            out_shape=jax.ShapeDtypeStruct((n, pairs, slots), bf),
            in_specs=[pl.BlockSpec(memory_space=pltpu.HBM)] * 2,
            out_specs=pl.BlockSpec(memory_space=pltpu.VMEM),
            scratch_shapes=[pltpu.SMEM((slab_sizes.shape[0],), jnp.int32)] * 2 + [
                pltpu.VMEM((pairs, packed), bf),
                dma((2,)),
            ],
            compiler_params=pltpu.CompilerParams(vmem_limit_bytes=211 << 18),
            cost_estimate=pl.CostEstimate(flops=0, bytes_accessed=2 << 20, transcendentals=0),
        )(slab_sizes, tau_ao)
        return pl.pallas_call(
            functools.partial(kernel, n, groups),
            out_shape=jax.ShapeDtypeStruct((pairs, LANES), f32),
            in_specs=[pl.BlockSpec(memory_space=pltpu.VMEM)] + [pl.BlockSpec(memory_space=pltpu.HBM)] * 2,
            out_specs=pl.BlockSpec(memory_space=pltpu.VMEM),
            scratch_shapes=[
                pltpu.VMEM((slabs, rows, width), bf),
                pltpu.VMEM((width, virtuals), f32),
                pltpu.VMEM((width, virtuals), bf),
                pltpu.VMEM((width, virtuals), bf),
                pltpu.VMEM((slots, virtuals), bf),
                pltpu.VMEM((slots, virtuals), bf),
                pltpu.VMEM((n, pairs, slots), bf),
                pltpu.VMEM((n, 2, 2, pairs, LANES), f32),
                pltpu.VMEM((n, 2, pairs, LANES), f32),
                pltpu.VMEM((n, pairs, LANES), f32),
                pltpu.VMEM((ending, 3, pairs, LANES), f32),
                pltpu.VMEM((n, pairs, LANES), f32),
                pltpu.VMEM((n, pairs, LANES), f32),
                dma((3,)),
            ] + [dma((n,))] * 6 + [dma((ending, 3))] * 2 + [dma((n,))] * 2,
            compiler_params=pltpu.CompilerParams(
                collective_id=0, has_side_effects=True, vmem_limit_bytes=211 << 18
            ),
            cost_estimate=pl.CostEstimate(flops=flops, bytes_accessed=4 << 20, transcendentals=0),
        )(amps, integrals, transform)

    return jax.shard_map(
        body,
        mesh=mesh,
        in_specs=(P("pair", None), P(), P("pair", "rep", None), P()),
        out_specs=P("pair", "rep"),
        check_vma=False,
    )
```

```python
import functools

import jax
import jax.numpy as jnp
from jax import lax
from jax.experimental import pallas as pl
from jax.experimental.pallas import tpu as pltpu
from jax.sharding import PartitionSpec as P

MESH = pl.DeviceIdType.MESH
LANES = 128
AHEAD = 3


def partner(me, slot, n):
    other, bit = 0, 1
    while bit < n:
        other += lax.rem(lax.div(me, bit) + lax.div(slot, bit), 2) * bit
        bit *= 2
    return other


def pick_kernel(n, slabs, sizes_in, tau_in, target, offsets, sizes, tau, load_sem):
    me, rep = lax.axis_index("pair"), lax.axis_index("rep")
    pairs, packed = tau.shape
    rows = target.shape[2] // slabs

    load_sizes = pltpu.make_async_copy(sizes_in, sizes, load_sem.at[0])
    load_tau = pltpu.make_async_copy(tau_in, tau, load_sem.at[1])
    load_sizes.start()
    load_tau.start()
    load_sizes.wait()

    def add_up(s, total):
        offsets[s] = total
        return total + sizes[s]

    lax.fori_loop(0, sizes.shape[0], add_up, jnp.int32(0))
    places = lax.broadcasted_iota(jnp.int32, (pairs, rows), 1) + rep * rows
    load_tau.wait()

    @pl.loop(0, n, unroll=4)
    def _(slot):
        dest = partner(me, slot, n)
        for q in range(slabs):
            slab = dest * slabs + q
            start = jnp.minimum(offsets[slab] + rep * rows, packed - 1)
            base = jnp.minimum(lax.div(start, LANES) * LANES, packed - 2 * LANES)
            window = tau[:, pl.ds(pl.multiple_of(base, LANES), 2 * LANES)].astype(jnp.float32)
            turned = pltpu.roll(window, lax.rem(2 * LANES - (start - base), 2 * LANES), 1)[:, :rows]
            kept = jnp.where(places < sizes[slab], turned, 0.0)
            target[slot, :, q * rows : (q + 1) * rows] = kept.astype(jnp.bfloat16)


def kernel(
    n, groups, amps_out, integrals_in, transform_in, out,
    integrals, transform, t_hi, t_lo, w_hi, w_lo, amps, part, core_in, x_in, rep_in, done, back,
    load_sem, amps_send, amps_recv, core_send, core_recv, x_send, x_recv, rep_send, rep_recv, back_send, back_recv,
):
    me, rep = lax.axis_index("pair"), lax.axis_index("rep")
    hi, lo = lax.div(rep, 2), lax.rem(rep, 2)
    near, far = hi * 2 + (1 - lo), (1 - hi) * 2 + lo
    both = (1 - hi) * 2 + (1 - lo)
    slabs, rows, width = integrals.shape

    load_own = pltpu.make_async_copy(amps_out.at[0], amps.at[0], load_sem.at[0])
    load_integrals = pltpu.make_async_copy(integrals_in, integrals, load_sem.at[1])
    load_transform = pltpu.make_async_copy(transform_in, transform, load_sem.at[2])
    load_own.start()
    load_transform.start()
    load_integrals.start()

    barrier = pltpu.get_barrier_semaphore()

    @pl.loop(1, n)
    def _(slot):
        other = partner(me, slot, n)
        pl.semaphore_signal(barrier, inc=1, device_id=(other, rep), device_id_type=MESH)

    pl.semaphore_signal(barrier, inc=1, device_id=(me, near), device_id_type=MESH)
    pl.semaphore_signal(barrier, inc=1, device_id=(me, far), device_id_type=MESH)
    pl.semaphore_signal(barrier, inc=1, device_id=(me, both), device_id_type=MESH)

    def send_amps(slot):
        other = partner(me, slot, n)
        return pltpu.make_async_remote_copy(
            src_ref=amps_out.at[slot], dst_ref=amps.at[slot],
            send_sem=amps_send.at[slot], recv_sem=amps_recv.at[slot],
            device_id=(other, rep), device_id_type=MESH,
        )

    def send_core(slot):
        return pltpu.make_async_remote_copy(
            src_ref=part.at[slot, 1 - lo], dst_ref=core_in.at[slot],
            send_sem=core_send.at[slot], recv_sem=core_recv.at[slot],
            device_id=(me, near), device_id_type=MESH,
        )

    def send_x(slot):
        return pltpu.make_async_remote_copy(
            src_ref=part.at[slot, lo, 1 - hi], dst_ref=x_in.at[slot],
            send_sem=x_send.at[slot], recv_sem=x_recv.at[slot],
            device_id=(me, far), device_id_type=MESH,
        )

    def send_direct(slot, way):
        other = (near, far, both)[way]
        at = slot - groups[-1][0]
        return pltpu.make_async_remote_copy(
            src_ref=part.at[slot, lax.rem(other, 2), lax.div(other, 2)], dst_ref=rep_in.at[at, way],
            send_sem=rep_send.at[at, way], recv_sem=rep_recv.at[at, way],
            device_id=(me, other), device_id_type=MESH,
        )

    def send_back(slot):
        owner = partner(me, slot, n)
        return pltpu.make_async_remote_copy(
            src_ref=done.at[slot], dst_ref=back.at[slot],
            send_sem=back_send.at[slot], recv_sem=back_recv.at[slot],
            device_id=(owner, rep), device_id_type=MESH,
        )

    pl.semaphore_wait(barrier, n + 2)

    half = n // 2

    @pl.loop(half, half + AHEAD)
    def _(slot):
        send_amps(slot).start()

    @pl.loop(1, half)
    def _(slot):
        send_amps(slot).start()

    load_transform.wait()

    @pl.loop(0, width, step=256)
    def _(k):
        block = transform[pl.ds(k, 256), :]
        high = block.astype(jnp.bfloat16)
        t_hi[pl.ds(k, 256), :] = high
        t_lo[pl.ds(k, 256), :] = (block - high.astype(jnp.float32)).astype(jnp.bfloat16)

    load_integrals.wait()
    for at in range(0, t_hi.shape[1], 2 * LANES):
        flat = integrals[...].reshape(slabs * rows, width)
        columns = slice(at, at + 2 * LANES)
        w = jnp.dot(flat, t_lo[:, columns], preferred_element_type=jnp.float32)
        w += jnp.dot(flat, t_hi[:, columns], preferred_element_type=jnp.float32)
        high = w.astype(jnp.bfloat16)
        w_hi[:, columns] = high
        w_lo[:, columns] = (w - high.astype(jnp.float32)).astype(jnp.bfloat16)

    load_own.wait()

    def multiply(first, last, direct):
        @pl.loop(first, last)
        def _(slot):
            @pl.when(slot >= 1)
            def _():
                send_amps(slot).wait_recv()

            @pl.when(jnp.logical_and(slot >= half, slot < n - AHEAD))
            def _():
                send_amps(slot).wait_send()
                send_amps(slot + AHEAD).start()

            block = amps[slot]
            for h in range(2):
                columns = slice(h * 2 * LANES, (h + 1) * 2 * LANES)
                p = jnp.dot(block, w_lo[:, columns], preferred_element_type=jnp.float32)
                p += jnp.dot(block, w_hi[:, columns], preferred_element_type=jnp.float32)
                part[slot, 0, h] = p[:, :LANES]
                part[slot, 1, h] = p[:, LANES:]
            if direct:
                for way in (1, 2, 0):
                    send_direct(slot, way).start()
            else:
                send_core(slot).start()

    def sum_core(first, last):
        @pl.loop(first, last)
        def _(slot):
            send_core(slot).wait_recv()
            part[slot, lo, 1 - hi] = part[slot, lo, 1 - hi] + core_in[slot, 1 - hi]
            send_x(slot).start()

    def sum_x(first, last):
        @pl.loop(first, last)
        def _(slot):
            send_x(slot).wait_recv()
            done[slot] = part[slot, lo, hi] + core_in[slot, hi] + x_in[slot]

            @pl.when(slot >= 1)
            def _():
                send_back(slot).start()

    def sum_direct(first, last):
        @pl.loop(first, last)
        def _(slot):
            total = part[slot, lo, hi]
            for way in range(3):
                send_direct(slot, way).wait_recv()
                total = total + rep_in[slot - first, way]
            done[slot] = total
            send_back(slot).start()

    for at, group in enumerate(groups):
        direct = at == len(groups) - 1
        first, last = group
        if at and not direct:
            multiply(first, first + 1, direct)
            sum_x(*groups[at - 1])
            multiply(first + 1, last, direct)
        else:
            multiply(first, last, direct)
            if at:
                sum_x(*groups[at - 1])
        if not direct:
            sum_core(*group)
    sum_direct(*groups[-1])

    out[...] = done[0]

    @pl.loop(1, n)
    def _(slot):
        send_back(slot).wait_recv()
        out[...] = out[...] + back[slot]

    @pl.loop(0, n)
    def _(slot):
        @pl.when(slot >= 1)
        def _():
            send_back(slot).wait_send()

        @pl.when(jnp.logical_or(jnp.logical_and(slot >= 1, slot < half), slot >= n - AHEAD))
        def _():
            send_amps(slot).wait_send()

        @pl.when(slot < groups[-1][0])
        def _():
            send_core(slot).wait_send()
            send_x(slot).wait_send()

        @pl.when(slot >= groups[-1][0])
        def _():
            for way in range(3):
                send_direct(slot, way).wait_send()


def solution(mesh):
    n, reps = mesh.shape["pair"], mesh.shape["rep"]

    def body(tau_ao, slab_sizes, integrals, transform):
        pairs, packed = tau_ao.shape
        slabs, rows, width = integrals.shape
        virtuals = transform.shape[1]
        assert reps == 4 and rows == LANES and virtuals == reps * LANES
        slots = slabs * rows
        half = n // 2
        groups = [(0, half)] + [(at, min(at + AHEAD, n)) for at in range(half, n, AHEAD)]
        ending = groups[-1][1] - groups[-1][0]
        bf, f32, dma = jnp.bfloat16, jnp.float32, pltpu.SemaphoreType.DMA
        flops = 4 * slots * width * virtuals + 4 * n * pairs * slots * virtuals
        amps = pl.pallas_call(
            functools.partial(pick_kernel, n, slabs),
            out_shape=jax.ShapeDtypeStruct((n, pairs, slots), bf),
            in_specs=[pl.BlockSpec(memory_space=pltpu.HBM)] * 2,
            out_specs=pl.BlockSpec(memory_space=pltpu.VMEM),
            scratch_shapes=[pltpu.SMEM((slab_sizes.shape[0],), jnp.int32)] * 2 + [
                pltpu.VMEM((pairs, packed), bf),
                dma((2,)),
            ],
            compiler_params=pltpu.CompilerParams(vmem_limit_bytes=211 << 18),
            cost_estimate=pl.CostEstimate(flops=0, bytes_accessed=2 << 20, transcendentals=0),
        )(slab_sizes, tau_ao)
        return pl.pallas_call(
            functools.partial(kernel, n, groups),
            out_shape=jax.ShapeDtypeStruct((pairs, LANES), f32),
            in_specs=[pl.BlockSpec(memory_space=pltpu.VMEM)] + [pl.BlockSpec(memory_space=pltpu.HBM)] * 2,
            out_specs=pl.BlockSpec(memory_space=pltpu.VMEM),
            scratch_shapes=[
                pltpu.VMEM((slabs, rows, width), bf),
                pltpu.VMEM((width, virtuals), f32),
                pltpu.VMEM((width, virtuals), bf),
                pltpu.VMEM((width, virtuals), bf),
                pltpu.VMEM((slots, virtuals), bf),
                pltpu.VMEM((slots, virtuals), bf),
                pltpu.VMEM((n, pairs, slots), bf),
                pltpu.VMEM((n, 2, 2, pairs, LANES), f32),
                pltpu.VMEM((n, 2, pairs, LANES), f32),
                pltpu.VMEM((n, pairs, LANES), f32),
                pltpu.VMEM((ending, 3, pairs, LANES), f32),
                pltpu.VMEM((n, pairs, LANES), f32),
                pltpu.VMEM((n, pairs, LANES), f32),
                dma((3,)),
            ] + [dma((n,))] * 6 + [dma((ending, 3))] * 2 + [dma((n,))] * 2,
            compiler_params=pltpu.CompilerParams(
                collective_id=0, has_side_effects=True, vmem_limit_bytes=211 << 18
            ),
            cost_estimate=pl.CostEstimate(flops=flops, bytes_accessed=4 << 20, transcendentals=0),
        )(amps, integrals, transform)

    return jax.shard_map(
        body,
        mesh=mesh,
        in_specs=(P("pair", None), P(), P("pair", "rep", None), P()),
        out_specs=P("pair", "rep"),
        check_vma=False,
    )
```

```python
import functools

import jax
import jax.numpy as jnp
from jax import lax
from jax.experimental import pallas as pl
from jax.experimental.pallas import tpu as pltpu
from jax.sharding import PartitionSpec as P

MESH = pl.DeviceIdType.MESH
LANES = 128
AHEAD = 3


def partner(me, slot, n):
    other, bit = 0, 1
    while bit < n:
        other += lax.rem(lax.div(me, bit) + lax.div(slot, bit), 2) * bit
        bit *= 2
    return other


def pick_kernel(n, slabs, sizes_in, tau_in, target, offsets, sizes, tau, load_sem):
    me, rep = lax.axis_index("pair"), lax.axis_index("rep")
    pairs, packed = tau.shape
    rows = target.shape[2] // slabs

    load_sizes = pltpu.make_async_copy(sizes_in, sizes, load_sem.at[0])
    load_tau = pltpu.make_async_copy(tau_in, tau, load_sem.at[1])
    load_sizes.start()
    load_tau.start()
    load_sizes.wait()

    def add_up(s, total):
        offsets[s] = total
        return total + sizes[s]

    lax.fori_loop(0, sizes.shape[0], add_up, jnp.int32(0))
    places = lax.broadcasted_iota(jnp.int32, (pairs, rows), 1) + rep * rows
    load_tau.wait()

    @pl.loop(0, n, unroll=4)
    def _(slot):
        dest = partner(me, slot, n)
        for q in range(slabs):
            slab = dest * slabs + q
            start = jnp.minimum(offsets[slab] + rep * rows, packed - 1)
            base = jnp.minimum(lax.div(start, LANES) * LANES, packed - 2 * LANES)
            window = tau[:, pl.ds(pl.multiple_of(base, LANES), 2 * LANES)].astype(jnp.float32)
            turned = pltpu.roll(window, lax.rem(2 * LANES - (start - base), 2 * LANES), 1)[:, :rows]
            kept = jnp.where(places < sizes[slab], turned, 0.0)
            target[slot, :, q * rows : (q + 1) * rows] = kept.astype(jnp.bfloat16)


def kernel(
    n, groups, amps_out, integrals_in, transform_in, out,
    integrals, transform, t_hi, t_lo, w_hi, w_lo, amps, part, core_in, x_in, rep_in, done, back,
    load_sem, amps_send, amps_recv, core_send, core_recv, x_send, x_recv, rep_send, rep_recv, back_send, back_recv,
):
    me, rep = lax.axis_index("pair"), lax.axis_index("rep")
    hi, lo = lax.div(rep, 2), lax.rem(rep, 2)
    near, far = hi * 2 + (1 - lo), (1 - hi) * 2 + lo
    both = (1 - hi) * 2 + (1 - lo)
    slabs, rows, width = integrals.shape

    load_own = pltpu.make_async_copy(amps_out.at[0], amps.at[0], load_sem.at[0])
    load_integrals = pltpu.make_async_copy(integrals_in, integrals, load_sem.at[1])
    load_transform = pltpu.make_async_copy(transform_in, transform, load_sem.at[2])
    load_own.start()
    load_transform.start()
    load_integrals.start()

    barrier = pltpu.get_barrier_semaphore()

    @pl.loop(1, n)
    def _(slot):
        other = partner(me, slot, n)
        pl.semaphore_signal(barrier, inc=1, device_id=(other, rep), device_id_type=MESH)

    pl.semaphore_signal(barrier, inc=1, device_id=(me, near), device_id_type=MESH)
    pl.semaphore_signal(barrier, inc=1, device_id=(me, far), device_id_type=MESH)
    pl.semaphore_signal(barrier, inc=1, device_id=(me, both), device_id_type=MESH)

    def send_amps(slot):
        other = partner(me, slot, n)
        return pltpu.make_async_remote_copy(
            src_ref=amps_out.at[slot], dst_ref=amps.at[slot],
            send_sem=amps_send.at[slot], recv_sem=amps_recv.at[slot],
            device_id=(other, rep), device_id_type=MESH,
        )

    def send_core(slot):
        return pltpu.make_async_remote_copy(
            src_ref=part.at[slot, 1 - lo], dst_ref=core_in.at[slot],
            send_sem=core_send.at[slot], recv_sem=core_recv.at[slot],
            device_id=(me, near), device_id_type=MESH,
        )

    def send_x(slot):
        return pltpu.make_async_remote_copy(
            src_ref=part.at[slot, lo, 1 - hi], dst_ref=x_in.at[slot],
            send_sem=x_send.at[slot], recv_sem=x_recv.at[slot],
            device_id=(me, far), device_id_type=MESH,
        )

    def send_direct(slot, way):
        other = (near, far, both)[way]
        at = slot - groups[-1][0]
        return pltpu.make_async_remote_copy(
            src_ref=part.at[slot, lax.rem(other, 2), lax.div(other, 2)], dst_ref=rep_in.at[at, way],
            send_sem=rep_send.at[at, way], recv_sem=rep_recv.at[at, way],
            device_id=(me, other), device_id_type=MESH,
        )

    def send_back(slot):
        owner = partner(me, slot, n)
        return pltpu.make_async_remote_copy(
            src_ref=done.at[slot], dst_ref=back.at[slot],
            send_sem=back_send.at[slot], recv_sem=back_recv.at[slot],
            device_id=(owner, rep), device_id_type=MESH,
        )

    pl.semaphore_wait(barrier, n + 2)

    half = n // 2

    @pl.loop(half, half + AHEAD)
    def _(slot):
        send_amps(slot).start()

    @pl.loop(1, half)
    def _(slot):
        send_amps(slot).start()

    load_transform.wait()

    @pl.loop(0, width, step=256)
    def _(k):
        block = transform[pl.ds(k, 256), :]
        high = block.astype(jnp.bfloat16)
        t_hi[pl.ds(k, 256), :] = high
        t_lo[pl.ds(k, 256), :] = (block - high.astype(jnp.float32)).astype(jnp.bfloat16)

    load_integrals.wait()
    for at in range(0, t_hi.shape[1], 2 * LANES):
        flat = integrals[...].reshape(slabs * rows, width)
        columns = slice(at, at + 2 * LANES)
        w = jnp.dot(flat, t_lo[:, columns], preferred_element_type=jnp.float32)
        w += jnp.dot(flat, t_hi[:, columns], preferred_element_type=jnp.float32)
        high = w.astype(jnp.bfloat16)
        w_hi[:, columns] = high
        w_lo[:, columns] = (w - high.astype(jnp.float32)).astype(jnp.bfloat16)

    load_own.wait()

    def multiply(first, last, direct):
        @pl.loop(first, last, unroll=2 - (last - first) % 2)
        def _(slot):
            @pl.when(slot >= 1)
            def _():
                send_amps(slot).wait_recv()

            @pl.when(jnp.logical_and(slot >= half, slot < n - AHEAD))
            def _():
                send_amps(slot).wait_send()
                send_amps(slot + AHEAD).start()

            block = amps[slot]
            for h in range(2):
                columns = slice(h * 2 * LANES, (h + 1) * 2 * LANES)
                p = jnp.dot(block, w_lo[:, columns], preferred_element_type=jnp.float32)
                p += jnp.dot(block, w_hi[:, columns], preferred_element_type=jnp.float32)
                part[slot, 0, h] = p[:, :LANES]
                part[slot, 1, h] = p[:, LANES:]
            if direct:
                for way in (1, 2, 0):
                    send_direct(slot, way).start()
            else:
                send_core(slot).start()

    def sum_core(first, last):
        @pl.loop(first, last, unroll=2 - (last - first) % 2)
        def _(slot):
            send_core(slot).wait_recv()
            part[slot, lo, 1 - hi] = part[slot, lo, 1 - hi] + core_in[slot, 1 - hi]
            send_x(slot).start()

    def sum_x(first, last):
        @pl.loop(first, last, unroll=2 - (last - first) % 2)
        def _(slot):
            send_x(slot).wait_recv()
            done[slot] = part[slot, lo, hi] + core_in[slot, hi] + x_in[slot]

            @pl.when(slot >= 1)
            def _():
                send_back(slot).start()

    def sum_direct(first, last):
        @pl.loop(first, last, unroll=2 - (last - first) % 2)
        def _(slot):
            total = part[slot, lo, hi]
            for way in range(3):
                send_direct(slot, way).wait_recv()
                total = total + rep_in[slot - first, way]
            done[slot] = total
            send_back(slot).start()

    for at, group in enumerate(groups):
        direct = at == len(groups) - 1
        first, last = group
        if at and not direct:
            multiply(first, first + 1, direct)
            sum_x(*groups[at - 1])
            multiply(first + 1, last, direct)
        else:
            multiply(first, last, direct)
            if at:
                sum_x(*groups[at - 1])
        if not direct:
            sum_core(*group)
    sum_direct(*groups[-1])

    out[...] = done[0]

    @pl.loop(1, n)
    def _(slot):
        send_back(slot).wait_recv()
        out[...] = out[...] + back[slot]

    @pl.loop(0, n)
    def _(slot):
        @pl.when(slot >= 1)
        def _():
            send_back(slot).wait_send()

        @pl.when(jnp.logical_or(jnp.logical_and(slot >= 1, slot < half), slot >= n - AHEAD))
        def _():
            send_amps(slot).wait_send()

        @pl.when(slot < groups[-1][0])
        def _():
            send_core(slot).wait_send()
            send_x(slot).wait_send()

        @pl.when(slot >= groups[-1][0])
        def _():
            for way in range(3):
                send_direct(slot, way).wait_send()


def solution(mesh):
    n, reps = mesh.shape["pair"], mesh.shape["rep"]

    def body(tau_ao, slab_sizes, integrals, transform):
        pairs, packed = tau_ao.shape
        slabs, rows, width = integrals.shape
        virtuals = transform.shape[1]
        assert reps == 4 and rows == LANES and virtuals == reps * LANES
        slots = slabs * rows
        half = n // 2
        groups = [(0, half)] + [(at, min(at + AHEAD, n)) for at in range(half, n, AHEAD)]
        ending = groups[-1][1] - groups[-1][0]
        bf, f32, dma = jnp.bfloat16, jnp.float32, pltpu.SemaphoreType.DMA
        flops = 4 * slots * width * virtuals + 4 * n * pairs * slots * virtuals
        amps = pl.pallas_call(
            functools.partial(pick_kernel, n, slabs),
            out_shape=jax.ShapeDtypeStruct((n, pairs, slots), bf),
            in_specs=[pl.BlockSpec(memory_space=pltpu.HBM)] * 2,
            out_specs=pl.BlockSpec(memory_space=pltpu.VMEM),
            scratch_shapes=[pltpu.SMEM((slab_sizes.shape[0],), jnp.int32)] * 2 + [
                pltpu.VMEM((pairs, packed), bf),
                dma((2,)),
            ],
            compiler_params=pltpu.CompilerParams(vmem_limit_bytes=211 << 18),
            cost_estimate=pl.CostEstimate(flops=0, bytes_accessed=2 << 20, transcendentals=0),
        )(slab_sizes, tau_ao)
        return pl.pallas_call(
            functools.partial(kernel, n, groups),
            out_shape=jax.ShapeDtypeStruct((pairs, LANES), f32),
            in_specs=[pl.BlockSpec(memory_space=pltpu.VMEM)] + [pl.BlockSpec(memory_space=pltpu.HBM)] * 2,
            out_specs=pl.BlockSpec(memory_space=pltpu.VMEM),
            scratch_shapes=[
                pltpu.VMEM((slabs, rows, width), bf),
                pltpu.VMEM((width, virtuals), f32),
                pltpu.VMEM((width, virtuals), bf),
                pltpu.VMEM((width, virtuals), bf),
                pltpu.VMEM((slots, virtuals), bf),
                pltpu.VMEM((slots, virtuals), bf),
                pltpu.VMEM((n, pairs, slots), bf),
                pltpu.VMEM((n, 2, 2, pairs, LANES), f32),
                pltpu.VMEM((n, 2, pairs, LANES), f32),
                pltpu.VMEM((n, pairs, LANES), f32),
                pltpu.VMEM((ending, 3, pairs, LANES), f32),
                pltpu.VMEM((n, pairs, LANES), f32),
                pltpu.VMEM((n, pairs, LANES), f32),
                dma((3,)),
            ] + [dma((n,))] * 6 + [dma((ending, 3))] * 2 + [dma((n,))] * 2,
            compiler_params=pltpu.CompilerParams(
                collective_id=0, has_side_effects=True, vmem_limit_bytes=211 << 18
            ),
            cost_estimate=pl.CostEstimate(flops=flops, bytes_accessed=4 << 20, transcendentals=0),
        )(amps, integrals, transform)

    return jax.shard_map(
        body,
        mesh=mesh,
        in_specs=(P("pair", None), P(), P("pair", "rep", None), P()),
        out_specs=P("pair", "rep"),
        check_vma=False,
    )
```
